32 devices in a mesh: groups: 2 (over x), tm: 16 (over z, y, core).
Axes of the slice: x: 2, y: 2, z: 4, core: 2. Of those that a mesh axis runs over, the one named last changes fastest.
Arguments:
- observations: float32 [32, 8192], P(('groups', 'tm')), parts along dimension 0, may hold values from -6 to 6
- block_mask: int32 [32, 64], P(('groups', 'tm')), parts along dimension 0, may hold values 0 or 1
- block_of_sensor: int32 [8192], replicated, may hold values from 0 to 63
- sensor_basis: float32 [8192, 128], replicated, may hold values from -0.0625 to 0.0625
- noise_var: float32 [8192], replicated, may hold values from 0.25 to 1
- mode_rate: float32 [128], replicated, may hold values from 0.015 to 1
- mode_var: float32 [128], replicated, may hold values from 0.5 to 2
Outputs:
- field: float32 [32, 8192], P(('groups', 'tm')), parts along dimension 0
- variances: float32 [32, 256], P(('groups', 'tm')), parts along dimension 0
- misfit: float32 [2], P('groups'), parts along dimension 0
The draws below stay inside these ranges and needn't reach their ends.
There are 2 independent parts, one for each index of `groups`. The reference program is written for one: setup_inputs(seed, part) draws one part's arguments, and reference() takes and returns one part's arrays. A program takes and returns all parts, laid end to end along the dimension named above; an argument that names none is the same for every part. Nothing has to cross between parts.
All inputs are finite; a program needn't handle non-finite values. No bound on the sum of `block_mask` on one device may be relied on, other than what follows from the above.
Results may differ from the reference program's by a relative error of at most 0.0003.
Values sent between devices are 32-bit elements; how exact they have to be, the bound alone decides.
No kernel may reach another device: no remote copies, remote signals or barrier semaphores. Data moves between devices by JAX's collectives and lax.ppermute only.
A program may use at most 128 MiB of HBM per device.

```python
import math
import jax
import jax.numpy as jnp
from jax import lax

MODES = 128
SENSORS = 8192
BLOCKS = 64
STEPS = 16


def with_ends(drawn, own_key, low, high):
    spot = [jax.random.randint(jax.random.fold_in(own_key, axis), (), 0, length) for axis, length in enumerate(drawn.shape)]
    widest = drawn.shape.index(max(drawn.shape))
    neighbour = spot[:widest] + [(spot[widest] + 1) % drawn.shape[widest]] + spot[widest + 1:]
    return drawn.at[tuple(spot)].set(low).at[tuple(neighbour)].set(high)


def steps_of(stream_key, dims, split, low, high):
    def one(position, blocks):
        draws = jax.random.uniform(jax.random.fold_in(jax.random.fold_in(stream_key, 6), position), (blocks,), jnp.float32, low / len(split), high / len(split))
        return jnp.repeat(jnp.exp(draws), dims[position] // blocks).reshape((-1,) + (1,) * (len(dims) - position - 1))

    level = one(*split[0])
    for cut in split[1:]:
        level = level * one(*cut)
    return level


def gaussian(own_key, shape, scale, reach, shards=(), kind=jnp.bfloat16):
    drawn = jax.random.normal(own_key, shape, jnp.float32) * scale
    if len(shards) > 0:
        drawn = steps_of(own_key, shape, shards, -0.22, 0.18) * drawn
    return jnp.clip(drawn, min=-reach, max=reach).astype(kind)


def setup_inputs(seed: int = 0, part: int = 0) -> dict:
    keys = jax.random.split(jax.random.key(seed), 8)
    part_keys = jax.random.split(jax.random.fold_in(keys[7], part), 8)
    observations = gaussian(part_keys[0], (STEPS, SENSORS), 1.0, 6.0, ((0, 16),), jnp.float32)
    block_mask = with_ends((jax.random.randint(part_keys[1], (STEPS, BLOCKS), 0, 4) < 3).astype(jnp.int32), jax.random.fold_in(part_keys[1], 1), 0, 1)
    block_of_sensor = with_ends(jax.random.randint(keys[2], (SENSORS,), 0, BLOCKS), jax.random.fold_in(keys[2], 1), 0, BLOCKS - 1).astype(jnp.int32)
    sensor_basis = gaussian(keys[3], (SENSORS, MODES), SENSORS ** -0.5, 0.0625, (), jnp.float32)
    noise_var = jnp.clip(jnp.exp(jax.random.uniform(keys[4], (SENSORS,), jnp.float32, math.log(0.25), math.log(1.0))), 0.25, 1.0)
    mode_rate = jnp.clip(jnp.exp(jax.random.uniform(keys[5], (MODES,), jnp.float32, math.log(0.015), math.log(1.0))), 0.015, 1.0)
    mode_var = jnp.clip(jnp.exp(jax.random.uniform(keys[6], (MODES,), jnp.float32, math.log(0.5), math.log(2.0))), 0.5, 2.0)
    return {"observations": observations, "block_mask": block_mask, "block_of_sensor": block_of_sensor, "sensor_basis": sensor_basis, "noise_var": noise_var, "mode_rate": mode_rate, "mode_var": mode_var}


def matmul(left, right):
    return jnp.dot(left.astype(jnp.float32), right.astype(jnp.float32), precision=lax.Precision.HIGHEST, preferred_element_type=jnp.float32)

def transition(mode_rate, mode_var):
    doubled = 2.0 * mode_rate
    damping = jnp.exp(-doubled)
    term_now = doubled * doubled * doubled / 6.0
    series = term_now
    for order in range(4, 15):
        term_now = term_now * doubled / order
        series = series + term_now
    q_value = mode_var * damping * series
    q_rate = mode_var * damping * (2.0 * doubled + series)
    q_cross = mode_var * damping * 2.0 * mode_rate * mode_rate
    root_value = jnp.sqrt(q_value)
    root_cross = q_cross / root_value
    root_rate = jnp.sqrt(q_value * q_rate - q_cross * q_cross) / root_value
    decay = jnp.exp(-mode_rate)
    return (decay * (1.0 + mode_rate), decay * mode_rate, -decay * mode_rate, decay * (1.0 - mode_rate), root_value, root_cross, root_rate, jnp.sqrt(mode_var))

def full_matrices(coefficients):
    f_vv, f_vr, f_rv, f_rr, root_value, root_cross, root_rate, sigma_vec = coefficients
    zero_block = jnp.zeros((f_vv.shape[0], f_vv.shape[0]), jnp.float32)
    trans_mat = jnp.block([[jnp.diag(f_vv), jnp.diag(f_vr)], [jnp.diag(f_rv), jnp.diag(f_rr)]])
    lower_mat = jnp.block([[jnp.diag(root_value), zero_block], [jnp.diag(root_cross), jnp.diag(root_rate)]])
    noise_mat = matmul(lower_mat, lower_mat.T)
    stationary = jnp.diag(jnp.concatenate([sigma_vec * sigma_vec, sigma_vec * sigma_vec]))
    return (trans_mat, noise_mat, stationary)

def reference(observations, block_mask, block_of_sensor, sensor_basis, noise_var, mode_rate, mode_var):
    coefficients = transition(mode_rate, mode_var)
    trans_mat, noise_mat, stationary = full_matrices(coefficients)
    onehot = (block_of_sensor[:, None] == jnp.arange(BLOCKS, dtype=jnp.int32)[None, :]).astype(jnp.float32)
    observed = matmul(block_mask.astype(jnp.float32), onehot.T)
    weights = observed / noise_var[None, :]

    def one_step(carry, inputs):
        mean_vec, covar = carry
        weight_row, reading_row, step_index = inputs
        info_mat = matmul(sensor_basis.T * weight_row[None, :], sensor_basis)
        grad_vec = matmul(weight_row * reading_row, sensor_basis)
        is_first = step_index == 0
        trans_eff = jnp.where(is_first, 0.0, trans_mat)
        noise_eff = jnp.where(is_first, stationary, noise_mat)
        pred_mean = matmul(trans_eff, mean_vec)
        pred_cov = matmul(matmul(trans_eff, covar), trans_eff.T) + noise_eff
        factor_p = jnp.linalg.cholesky(pred_cov)
        top_rows = factor_p[:MODES]
        inner = jnp.eye(2 * MODES, dtype=jnp.float32) + matmul(matmul(top_rows.T, info_mat), top_rows)
        factor_m = jnp.linalg.cholesky(inner)
        solved = jax.scipy.linalg.solve_triangular(factor_m, factor_p.T, lower=True)
        new_cov = matmul(solved.T, solved)
        new_mean = pred_mean + matmul(new_cov[:, :MODES], grad_vec - matmul(info_mat, pred_mean[:MODES]))
        return ((new_mean, new_cov), (new_mean, jnp.diagonal(new_cov)))
    start = (jnp.zeros((2 * MODES,), jnp.float32), jnp.zeros((2 * MODES, 2 * MODES), jnp.float32))
    step_ids = jnp.arange(STEPS, dtype=jnp.int32)
    unused, (means, variances) = lax.scan(one_step, start, (weights, observations, step_ids))
    field = matmul(means[:, :MODES], sensor_basis.T)
    misfit = jnp.sum(weights * (observations - field) ** 2) / (STEPS * SENSORS)
    return (field, variances, misfit.reshape(1))
```

```python
import functools

import jax
import jax.numpy as jnp
from jax import lax
from jax.experimental import pallas as pl
from jax.experimental.pallas import tpu as pltpu
from jax.sharding import PartitionSpec as P

BF16 = jnp.bfloat16
F32 = jnp.float32
AXIS = "tm"
LANES = 128
PIECES = 8
LIMIT_FIRST = 1.0e-2
LIMIT_LATER = 1.5e-3


def gather_rounds(count):
    bits = count.bit_length() - 1
    rounds = []
    top = bits
    if bits > 1 and (bits - 1) % 2 == 1:
        rounds.append((bits - 1, 1))
        top = bits - 1
    while top > 1:
        rounds.append((top - 2, 2))
        top -= 2
    if bits > 0:
        rounds.append((0, 1))
    return rounds


def exchange(part, count):
    rows = part
    for shift, width in gather_rounds(count):
        pieces = [rows]
        for digit in range(1, 1 << width):
            flip = digit << shift
            pieces.append(lax.ppermute(rows, AXIS, [(p, p ^ flip) for p in range(count)]))
        rows = jnp.concatenate(pieces, axis=0)
    return rows


def slot_of(offset, count, local):
    slot = 0
    stride = local
    for shift, width in gather_rounds(count):
        slot = slot + ((offset >> shift) & ((1 << width) - 1)) * stride
        stride = stride << width
    return slot


def transition(mode_rate, mode_var):
    doubled = 2.0 * mode_rate
    damping = jnp.exp(-doubled)
    term_now = doubled * doubled * doubled / 6.0
    series = term_now
    for order in range(4, 15):
        term_now = term_now * doubled / order
        series = series + term_now
    q_value = mode_var * damping * series
    q_rate = mode_var * damping * (2.0 * doubled + series)
    q_cross = mode_var * damping * 2.0 * mode_rate * mode_rate
    root_value = jnp.sqrt(q_value)
    root_cross = q_cross / root_value
    root_rate = jnp.sqrt(q_value * q_rate - q_cross * q_cross) / root_value
    decay = jnp.exp(-mode_rate)
    return (
        decay * (1.0 + mode_rate),
        decay * mode_rate,
        -decay * mode_rate,
        decay * (1.0 - mode_rate),
        root_value,
        root_cross,
        root_rate,
        jnp.sqrt(mode_var),
    )


def split(x):
    high = x.astype(BF16)
    return high, (x - high.astype(F32)).astype(BF16)


def wide(x):
    return jnp.concatenate(split(x), axis=1)


def twice(x):
    return jnp.concatenate([x, x], axis=0)


def dot(left, right):
    return jnp.dot(left, right, preferred_element_type=F32)


def dot_split(left_wide, right_twice):
    both = dot(left_wide, right_twice)
    half = both.shape[1] // 2
    return both[:, :half] + both[:, half:]


def prepare_kernel(basis_ref, noise_ref, rate_ref, var_ref, scaled_t_ref, scaled_ref, root_ref, coef_ref):
    sensors, modes = basis_ref.shape
    root_ref[...] = lax.rsqrt(noise_ref[...])
    for start in range(0, sensors, LANES):
        span = slice(start, start + LANES)
        turned = basis_ref[span, :].T * root_ref[:, span]
        high, low = split(turned)
        scaled_t_ref[:modes, span] = high
        scaled_t_ref[modes:, span] = low
        scaled_ref[span, :] = wide(turned.T)
    f_vv, f_vr, f_rv, f_rr, root_value, root_cross, root_rate, sigma_vec = transition(rate_ref[...], var_ref[...])
    rows = (
        f_vv,
        f_vr,
        f_rv,
        f_rr,
        root_value * root_value,
        root_value * root_cross,
        root_cross * root_cross + root_rate * root_rate,
        sigma_vec * sigma_vec,
    )
    coef_ref[...] = jnp.concatenate(rows, axis=0)


def filter_kernel(
    position_ref,
    arrived_ref,
    block_ref,
    scaled_t_ref,
    scaled_ref,
    root_ref,
    noise_ref,
    coef_ref,
    field_ref,
    variances_ref,
    misfit_ref,
    bound_ref,
    p_vv,
    p_vr,
    p_rv,
    p_rr,
    pred_mean,
    columns,
    lam_now,
    mask_rows,
    readings,
    grads,
    means,
    diagonals,
    bounds,
    row_sums,
    *,
    count,
    local,
    blocks,
):
    modes = scaled_t_ref.shape[0] // 2
    sensors = scaled_t_ref.shape[1]
    steps = arrived_ref.shape[0]
    position = position_ref[0]
    row_index = lax.broadcasted_iota(jnp.int32, (modes, modes), 0)
    col_index = lax.broadcasted_iota(jnp.int32, (modes, modes), 1)
    eye = jnp.where(row_index == col_index, 1.0, 0.0).astype(F32)

    def coef(k):
        return coef_ref[k : k + 1, :]

    def slot(step):
        return slot_of((step // local) ^ position, count, local) + step % local

    def diagonal(square):
        return jnp.sum(eye * square, axis=0, keepdims=True)

    masks = arrived_ref[:, sensors : sensors + blocks].astype(BF16)
    block_index = lax.broadcasted_iota(jnp.int32, (blocks, sensors), 0)
    onehot = jnp.where(block_index == block_ref[...], 1.0, 0.0).astype(BF16)
    mask_rows[...] = dot(masks, onehot)
    readings[...] = mask_rows[...] * arrived_ref[:, :sensors] * root_ref[...]
    y_split = jnp.concatenate(split(readings[...]), axis=0)
    g_both = dot(y_split, scaled_ref[...])
    g_half = g_both[:, :modes] + g_both[:, modes:]
    grads[...] = g_half[:steps] + g_half[steps:]

    for k in range(4):
        columns[k] = jnp.broadcast_to(jnp.sum(eye * coef(k), axis=1, keepdims=True), (modes, modes))
    stationary = eye * coef(7)
    p_vv[...] = stationary
    p_rr[...] = stationary
    p_vr[...] = jnp.zeros((modes, modes), F32)
    p_rv[...] = jnp.zeros((modes, modes), F32)
    pred_mean[...] = jnp.zeros(pred_mean.shape, F32)
    bounds[...] = jnp.zeros(bounds.shape, F32)

    depth = sensors // PIECES

    def gram_piece(piece, at):
        span = slice(piece * depth, (piece + 1) * depth)
        left = scaled_t_ref[:modes, span] * mask_rows[pl.ds(at, 1), span].astype(BF16)
        return dot(left, scaled_ref[span, :])

    def gram_finish(total):
        cross = total[:, modes:]
        lam_now[...] = total[:, :modes] + cross + cross.T

    first = gram_piece(0, slot(0))
    for piece in range(1, PIECES):
        first = first + gram_piece(piece, slot(0))
    gram_finish(first)

    def one_step(step, carry):
        here = slot(step)
        ahead = slot(jnp.minimum(step + 1, steps - 1))
        lam = lam_now[...]
        pred_vv = p_vv[...]
        pred_rv = p_rv[...]
        pred_rr = p_rr[...]
        lam_wide = wide(lam)
        lam_p = dot_split(lam_wide, twice(wide(pred_vv)))
        cross = dot_split(lam_wide, twice(wide(p_vr[...])))
        total = gram_piece(0, ahead) + gram_piece(1, ahead)
        scale = 1.0 / (1.0 + diagonal(lam) * diagonal(pred_vv))
        rest = eye * (1.0 - scale) - lam_p * scale
        scaled_p = jnp.concatenate([pred_vv * scale, pred_rv * scale], axis=0)
        second = dot_split(wide(jnp.concatenate([rest, scaled_p], axis=0)), twice(wide(rest)))
        total = total + (gram_piece(2, ahead) + gram_piece(3, ahead))
        rest2 = second[:modes]
        cols1 = scaled_p + second[modes:]
        rest2_high = rest2.astype(BF16)
        cross_high, cross_low = split(cross)
        third = dot(
            jnp.concatenate([rest2_high, cols1.astype(BF16)], axis=0),
            jnp.concatenate([rest2_high, cross_high], axis=1),
        )
        total = total + (gram_piece(4, ahead) + gram_piece(5, ahead))
        rest4 = third[:modes, :modes]
        rest2_cross = third[:modes, modes:]
        cols_add = third[modes:, :modes]
        cols2 = cols1 + cols_add
        cols2_high, cols2_low = split(cols2)
        cols3 = cols2 + dot(cols2_high, rest4.astype(BF16))
        cross_wide = jnp.concatenate([cross_high, cross_low], axis=1)
        taken = dot_split(
            jnp.concatenate([cols2_high[modes:], cols2_low[modes:]], axis=1), twice(cross_wide)
        ) + dot(cols_add[modes:].astype(BF16), rest2_cross.astype(BF16))
        total = total + (gram_piece(6, ahead) + gram_piece(7, ahead))
        c_rr = pred_rr - taken
        c_vv = cols3[:modes]
        c_rv = cols3[modes:]
        c_vr = c_rv.T

        pull = grads[pl.ds(here, 1), :] - jnp.sum(lam * pred_mean[0], axis=0, keepdims=True)
        mean_v = pred_mean[0] + jnp.sum(c_vv * pull, axis=1, keepdims=True)
        mean_r = pred_mean[1] + jnp.sum(c_rv * pull, axis=1, keepdims=True)
        means[pl.ds(here, 1), :] = diagonal(mean_v)
        diagonals[pl.ds(here, 1), :] = jnp.concatenate([diagonal(c_vv), diagonal(c_rr)], axis=1)
        bounds[pl.ds(jnp.minimum(step, 1), 1), :] = jnp.maximum(
            bounds[pl.ds(jnp.minimum(step, 1), 1), :], jnp.sum(rest4 * rest4, axis=0, keepdims=True)
        )

        a, b, c, d = columns[0], columns[1], columns[2], columns[3]
        pred_mean[0] = a * mean_v + b * mean_r
        pred_mean[1] = c * mean_v + d * mean_r
        g_vv = a * c_vv + b * c_rv
        g_vr = a * c_vr + b * c_rr
        g_rv = c * c_vv + d * c_rv
        g_rr = c * c_vr + d * c_rr
        p_vv[...] = g_vv * coef(0) + g_vr * coef(1) + eye * coef(4)
        p_rv[...] = g_rv * coef(0) + g_rr * coef(1) + eye * coef(5)
        p_vr[...] = g_vv * coef(2) + g_vr * coef(3) + eye * coef(5)
        p_rr[...] = g_rv * coef(2) + g_rr * coef(3) + eye * coef(6)
        gram_finish(total)
        return carry

    lax.fori_loop(0, steps, one_step, 0)

    m_high, m_low = split(means[...])
    m_split = jnp.concatenate(
        [jnp.concatenate([m_high, m_high], axis=1), jnp.concatenate([m_low, m_low], axis=1)], axis=0
    )
    f_both = dot(m_split, scaled_t_ref[...])
    scaled_field = f_both[:steps] + f_both[steps:]
    field_ref[...] = scaled_field[:local] * (root_ref[...] * noise_ref[...])
    variances_ref[...] = diagonals[:local, :]
    gap = readings[...] - mask_rows[...] * scaled_field
    squares = gap * gap
    row_sums[...] = jnp.sum(squares.reshape(steps, sensors // LANES, LANES), axis=1)

    def add_row(step, total):
        return total + row_sums[pl.ds(slot(step), 1), :]

    lane_total = lax.fori_loop(0, steps, add_row, jnp.zeros((1, LANES), F32))
    misfit_ref[...] = jnp.sum(lane_total, axis=1, keepdims=True) / (steps * sensors)
    worst_first = jnp.sum(bounds[0:1], axis=1, keepdims=True) / (LIMIT_FIRST * LIMIT_FIRST)
    worst_later = jnp.sum(bounds[1:2], axis=1, keepdims=True) / (LIMIT_LATER * LIMIT_LATER)
    bound_ref[...] = jnp.maximum(worst_first, worst_later)


def matmul(left, right):
    return jnp.dot(left, right, precision=lax.Precision.HIGHEST, preferred_element_type=F32)


def careful(order, local, arrived, block_of_sensor, sensor_basis, noise_var, mode_rate, mode_var):
    sensors, modes = sensor_basis.shape
    blocks = arrived.shape[1] - sensors
    in_time = arrived[order]
    observations = in_time[:, :sensors]
    block_mask = in_time[:, sensors:]
    steps = observations.shape[0]
    f_vv, f_vr, f_rv, f_rr, root_value, root_cross, root_rate, sigma_vec = transition(mode_rate, mode_var)
    zero = jnp.zeros((modes, modes), F32)
    trans_mat = jnp.block([[jnp.diag(f_vv), jnp.diag(f_vr)], [jnp.diag(f_rv), jnp.diag(f_rr)]])
    lower_mat = jnp.block([[jnp.diag(root_value), zero], [jnp.diag(root_cross), jnp.diag(root_rate)]])
    noise_mat = matmul(lower_mat, lower_mat.T)
    stationary = jnp.diag(jnp.concatenate([sigma_vec * sigma_vec, sigma_vec * sigma_vec]))
    onehot = (block_of_sensor[:, None] == jnp.arange(blocks, dtype=jnp.int32)[None, :]).astype(F32)
    weights = matmul(block_mask, onehot.T) / noise_var[None, :]

    def one_step(carry, inputs):
        mean_vec, covar = carry
        weight_row, reading_row, step = inputs
        info_mat = matmul(sensor_basis.T * weight_row[None, :], sensor_basis)
        grad_vec = matmul((weight_row * reading_row)[None, :], sensor_basis)[0]
        trans_eff = jnp.where(step == 0, 0.0, trans_mat)
        noise_eff = jnp.where(step == 0, stationary, noise_mat)
        pred_mean = matmul(trans_eff, mean_vec[:, None])[:, 0]
        pred_cov = matmul(matmul(trans_eff, covar), trans_eff.T) + noise_eff
        factor_p = jnp.linalg.cholesky(pred_cov)
        top_rows = factor_p[:modes]
        inner = jnp.eye(2 * modes, dtype=F32) + matmul(matmul(top_rows.T, info_mat), top_rows)
        factor_m = jnp.linalg.cholesky(inner)
        solved = jax.scipy.linalg.solve_triangular(factor_m, factor_p.T, lower=True)
        new_cov = matmul(solved.T, solved)
        pull = grad_vec - matmul(info_mat, pred_mean[:modes, None])[:, 0]
        new_mean = pred_mean + matmul(new_cov[:, :modes], pull[:, None])[:, 0]
        return ((new_mean, new_cov), (new_mean, jnp.diagonal(new_cov)))

    start = (jnp.zeros((2 * modes,), F32), jnp.zeros((2 * modes, 2 * modes), F32))
    step_ids = jnp.arange(steps, dtype=jnp.int32)
    _, (means, variances) = lax.scan(one_step, start, (weights, observations, step_ids))
    field = matmul(means[:, :modes], sensor_basis.T)
    misfit = jnp.sum(weights * (observations - field) ** 2) / (steps * sensors)
    own = lax.axis_index(AXIS) * local
    own_field = lax.dynamic_slice_in_dim(field, own, local, 0)
    own_variances = lax.dynamic_slice_in_dim(variances, own, local, 0)
    return (own_field, own_variances, misfit.reshape(1, 1))


def in_vmem(count):
    return [pl.BlockSpec(memory_space=pltpu.VMEM)] * count


def on_device(observations, block_mask, block_of_sensor, sensor_basis, noise_var, mode_rate, mode_var):
    local, sensors = observations.shape
    modes = sensor_basis.shape[1]
    blocks = block_mask.shape[1]
    count = lax.axis_size(AXIS)
    steps = count * local
    noise_row = noise_var.reshape(1, sensors)
    position = lax.axis_index(AXIS).astype(jnp.int32)

    arrived = exchange(jnp.concatenate([observations, block_mask.astype(F32)], axis=1), count)

    scaled_t, scaled, root, coefs = pl.pallas_call(
        prepare_kernel,
        out_shape=(
            jax.ShapeDtypeStruct((2 * modes, sensors), BF16),
            jax.ShapeDtypeStruct((sensors, 2 * modes), BF16),
            jax.ShapeDtypeStruct((1, sensors), F32),
            jax.ShapeDtypeStruct((8, modes), F32),
        ),
        in_specs=in_vmem(4),
        out_specs=tuple(in_vmem(4)),
        compiler_params=pltpu.CompilerParams(vmem_limit_bytes=24 * 2**20),
        cost_estimate=pl.CostEstimate(flops=2 * sensors * modes, bytes_accessed=12 * sensors * modes, transcendentals=sensors),
        name="prepare",
    )(sensor_basis, noise_row, mode_rate.reshape(1, modes), mode_var.reshape(1, modes))

    square = pltpu.VMEM((modes, modes), F32)
    field, variances, misfit, bound = pl.pallas_call(
        functools.partial(filter_kernel, count=count, local=local, blocks=blocks),
        out_shape=(
            jax.ShapeDtypeStruct((local, sensors), F32),
            jax.ShapeDtypeStruct((local, 2 * modes), F32),
            jax.ShapeDtypeStruct((1, 1), F32),
            jax.ShapeDtypeStruct((1, 1), F32),
        ),
        in_specs=[pl.BlockSpec(memory_space=pltpu.SMEM)] + in_vmem(7),
        out_specs=tuple(in_vmem(4)),
        scratch_shapes=[
            square,
            square,
            square,
            square,
            pltpu.VMEM((2, modes, modes), F32),
            pltpu.VMEM((4, modes, modes), F32),
            square,
            pltpu.VMEM((steps, sensors), F32),
            pltpu.VMEM((steps, sensors), F32),
            pltpu.VMEM((steps, modes), F32),
            pltpu.VMEM((steps, modes), F32),
            pltpu.VMEM((steps, 2 * modes), F32),
            pltpu.VMEM((8, modes), F32),
            pltpu.VMEM((steps, LANES), F32),
        ],
        compiler_params=pltpu.CompilerParams(vmem_limit_bytes=40 * 2**20),
        cost_estimate=pl.CostEstimate(flops=steps * sensors * modes * 512, bytes_accessed=8 * sensors * modes, transcendentals=0),
        name="filter",
    )(position.reshape(1), arrived, block_of_sensor.reshape(1, sensors), scaled_t, scaled, root, noise_row, coefs)

    step_ids = jnp.arange(steps, dtype=jnp.int32)
    order = slot_of((step_ids // local) ^ position, count, local) + step_ids % local
    field, variances, misfit = lax.cond(
        bound[0, 0] <= 1.0,
        lambda: (field, variances, misfit),
        lambda: careful(order, local, arrived, block_of_sensor, sensor_basis, noise_var, mode_rate, mode_var),
    )
    return (field, variances, misfit.reshape(1))


def solution(mesh):
    in_specs = (P(("groups", "tm"), None), P(("groups", "tm"), None), P(), P(), P(), P(), P())
    out_specs = (P(("groups", "tm"), None), P(("groups", "tm"), None), P("groups"))
    return jax.shard_map(on_device, mesh=mesh, in_specs=in_specs, out_specs=out_specs, check_vma=False)
```

```python
import functools

import jax
import jax.numpy as jnp
from jax import lax
from jax.experimental import pallas as pl
from jax.experimental.pallas import tpu as pltpu
from jax.sharding import PartitionSpec as P

BF16 = jnp.bfloat16
F32 = jnp.float32
AXIS = "tm"
LANES = 128
PIECES = 8
COPIES = 8
LIMIT_FIRST = 1.0e-2
LIMIT_LATER = 1.5e-3


def gather_rounds(count):
    bits = count.bit_length() - 1
    rounds = []
    top = bits
    if bits > 1 and (bits - 1) % 2 == 1:
        rounds.append((bits - 1, 1))
        top = bits - 1
    while top > 1:
        rounds.append((top - 2, 2))
        top -= 2
    if bits > 0:
        rounds.append((0, 1))
    return rounds


def swap(array, flip, count):
    return lax.ppermute(array, AXIS, [(p, p ^ flip) for p in range(count)])


def pack(observations, block_mask):
    local, sensors = observations.shape
    mask_row = jnp.pad(block_mask.astype(F32), ((0, 0), (0, LANES - block_mask.shape[1])))
    mask_tile = jnp.pad(mask_row.reshape(local, 1, LANES), ((0, 0), (0, 7), (0, 0)))
    return jnp.concatenate([observations.reshape(local, sensors // LANES, LANES), mask_tile], axis=1)


def exchange(observations, block_mask, count, early, late, seed):
    rounds = gather_rounds(count)
    pieces = [pack(observations, block_mask)]
    done = None
    for turn, (shift, width) in enumerate(rounds):
        flips = [digit << shift for digit in range(1, 1 << width)]
        rows = pieces[0] if turn == 0 else jnp.concatenate(pieces, axis=0)
        if turn == len(rounds) - 2:
            rows, seed = lax.optimization_barrier((rows, seed))
            seed = early(seed)
        if turn == len(rounds) - 1:
            rows, seed = lax.optimization_barrier((rows, seed))
            done = late(seed)
        if turn == 0:
            pieces = [rows] + [pack(swap(observations, flip, count), swap(block_mask, flip, count)) for flip in flips]
        else:
            pieces = [rows] + [swap(rows, flip, count) for flip in flips]
    return pieces, done


def slot_of(offset, count, local):
    slot = 0
    stride = local
    for shift, width in gather_rounds(count):
        slot = slot + ((offset >> shift) & ((1 << width) - 1)) * stride
        stride = stride << width
    return slot


def transition(mode_rate, mode_var):
    doubled = 2.0 * mode_rate
    damping = jnp.exp(-doubled)
    term_now = doubled * doubled * doubled / 6.0
    series = term_now
    for order in range(4, 15):
        term_now = term_now * doubled / order
        series = series + term_now
    q_value = mode_var * damping * series
    q_rate = mode_var * damping * (2.0 * doubled + series)
    q_cross = mode_var * damping * 2.0 * mode_rate * mode_rate
    root_value = jnp.sqrt(q_value)
    root_cross = q_cross / root_value
    root_rate = jnp.sqrt(q_value * q_rate - q_cross * q_cross) / root_value
    decay = jnp.exp(-mode_rate)
    return (
        decay * (1.0 + mode_rate),
        decay * mode_rate,
        -decay * mode_rate,
        decay * (1.0 - mode_rate),
        root_value,
        root_cross,
        root_rate,
        jnp.sqrt(mode_var),
    )


def split(x):
    high = x.astype(BF16)
    return high, (x - high.astype(F32)).astype(BF16)


def wide(x):
    return jnp.concatenate(split(x), axis=1)


def twice(x):
    return jnp.concatenate([x, x], axis=0)


def dot(left, right):
    return jnp.dot(left, right, preferred_element_type=F32)


def dot_split(left_wide, right_twice):
    both = dot(left_wide, right_twice)
    half = both.shape[1] // 2
    return both[:, :half] + both[:, half:]


def dot_three(left_wide, right):
    high, low = split(right)
    return dot(left_wide, twice(high)) + dot(left_wide[:, : high.shape[0]], low)


def prepare_kernel(
    basis_ref,
    block_ref,
    rate_ref,
    var_ref,
    scaled_t_ref,
    scaled_ref,
    onehot_ref,
    coef_ref,
    basis,
    arrivals,
):
    sensors, modes = basis_ref.shape
    depth = sensors // COPIES
    copies = []
    for part in range(COPIES):
        rows = pl.ds(part * depth, depth)
        copies.append(pltpu.make_async_copy(basis_ref.at[rows], basis.at[rows], arrivals.at[part]))
        copies[part].start()
    f_vv, f_vr, f_rv, f_rr, root_value, root_cross, root_rate, sigma_vec = transition(rate_ref[...], var_ref[...])
    rows = (
        f_vv,
        f_vr,
        f_rv,
        f_rr,
        root_value * root_value,
        root_value * root_cross,
        root_cross * root_cross + root_rate * root_rate,
        sigma_vec * sigma_vec,
    )
    coef_ref[...] = jnp.concatenate(rows, axis=0)
    block_index = lax.broadcasted_iota(jnp.int32, onehot_ref.shape, 0)
    onehot_ref[...] = jnp.where(block_index == block_ref[...], 1.0, 0.0).astype(BF16)
    for start in range(0, sensors, LANES):
        if start % depth == 0:
            copies[start // depth].wait()
        span = slice(start, start + LANES)
        chunk = basis[span, :]
        high, low = split(chunk.T)
        scaled_t_ref[:modes, span] = high
        scaled_t_ref[modes:, span] = low
        scaled_ref[span, :] = wide(chunk)


def filter_kernel(position_ref, *refs, count, local, blocks, parts):
    pieces = refs[:parts]
    (
        onehot_ref,
        scaled_t_ref,
        scaled_ref,
        noise_ref,
        coef_ref,
        field_ref,
        variances_ref,
        misfit_ref,
        bound_ref,
        p_vv,
        p_vr,
        p_rv,
        p_rr,
        pred_mean,
        columns,
        lam_now,
        root_ref,
        mask_rows,
        readings,
        grads,
        means,
        diagonals,
        bounds,
        row_sums,
    ) = refs[parts:]
    modes = scaled_t_ref.shape[0] // 2
    sensors = scaled_t_ref.shape[1]
    piece_rows = pieces[0].shape[0]
    steps = parts * piece_rows
    chunks = sensors // LANES
    position = position_ref[0]
    row_index = lax.broadcasted_iota(jnp.int32, (modes, modes), 0)
    col_index = lax.broadcasted_iota(jnp.int32, (modes, modes), 1)
    eye = jnp.where(row_index == col_index, 1.0, 0.0).astype(F32)

    def coef(k):
        return coef_ref[k : k + 1, :]

    def slot(step):
        return slot_of((step // local) ^ position, count, local) + step % local

    def diagonal(square):
        return jnp.sum(eye * square, axis=0, keepdims=True)

    root_ref[...] = lax.rsqrt(noise_ref[...])
    masks = jnp.concatenate([ref[:, chunks, :blocks] for ref in pieces], axis=0).astype(BF16)
    mask_rows[...] = dot(masks, onehot_ref[...])
    for chunk in range(chunks):
        span = slice(chunk * LANES, (chunk + 1) * LANES)
        rows = jnp.concatenate([ref[:, chunk, :] for ref in pieces], axis=0)
        readings[:, span] = mask_rows[:, span] * rows * root_ref[:, span]
    for k in range(4):
        columns[k] = jnp.broadcast_to(jnp.sum(eye * coef(k), axis=1, keepdims=True), (modes, modes))
    stationary = eye * coef(7)
    p_vv[...] = stationary
    p_rr[...] = stationary
    p_vr[...] = jnp.zeros((modes, modes), F32)
    p_rv[...] = jnp.zeros((modes, modes), F32)
    pred_mean[...] = jnp.zeros(pred_mean.shape, F32)
    bounds[...] = jnp.zeros(bounds.shape, F32)

    depth = sensors // PIECES

    def gram_piece(piece, at):
        span = slice(piece * depth, (piece + 1) * depth)
        left = scaled_t_ref[:modes, span] * mask_rows[pl.ds(at, 1), span].astype(BF16)
        return dot(left, scaled_ref[span, :])

    def gram_finish(total):
        cross = total[:, modes:]
        lam_now[...] = total[:, :modes] + cross + cross.T

    first_left = scaled_t_ref[:modes, :] * mask_rows[pl.ds(slot(0), 1), :].astype(BF16)
    y_high, y_low = split(readings[...])
    first = dot(jnp.concatenate([first_left, y_high, y_low], axis=0), scaled_ref[...])
    gram_finish(first[:modes])
    g_half = first[modes:, :modes] + first[modes:, modes:]
    grads[...] = g_half[:steps] + g_half[steps:]

    def one_step(step, carry):
        here = slot(step)
        ahead = slot(jnp.minimum(step + 1, steps - 1))
        lam = lam_now[...]
        pred_vv = p_vv[...]
        pred_rv = p_rv[...]
        pred_rr = p_rr[...]
        lam_wide = wide(lam)
        lam_p = dot_three(lam_wide, pred_vv)
        cross = dot_three(lam_wide, p_vr[...])
        total = gram_piece(0, ahead) + gram_piece(1, ahead)
        scale = 1.0 / (1.0 + diagonal(lam) * diagonal(pred_vv))
        rest = eye * (1.0 - scale) - lam_p * scale
        scaled_p = jnp.concatenate([pred_vv * scale, pred_rv * scale], axis=0)
        second = dot_split(wide(jnp.concatenate([rest, scaled_p], axis=0)), twice(wide(rest)))
        total = total + (gram_piece(2, ahead) + gram_piece(3, ahead))
        rest2 = second[:modes]
        cols1 = scaled_p + second[modes:]
        rest2_high = rest2.astype(BF16)
        cross_high, cross_low = split(cross)
        rest4 = dot(rest2_high, rest2_high).astype(BF16)
        rest2_cross = dot(rest2_high, cross_high)
        cols_add = dot(cols1.astype(BF16), rest2_high)
        total = total + (gram_piece(4, ahead) + gram_piece(5, ahead))
        cols2 = cols1 + cols_add
        cols2_high, cols2_low = split(cols2)
        cols3 = cols2 + dot(cols2_high, rest4)
        cross_wide = jnp.concatenate([cross_high, cross_low], axis=1)
        taken = dot_split(
            jnp.concatenate([cols2_high[modes:], cols2_low[modes:]], axis=1), twice(cross_wide)
        ) + dot(cols_add[modes:].astype(BF16), rest2_cross.astype(BF16))
        total = total + (gram_piece(6, ahead) + gram_piece(7, ahead))
        c_rr = pred_rr - taken
        c_vv = cols3[:modes]
        c_rv = cols3[modes:]
        c_vr = cols2[modes:].T + lax.dot_general(
            rest4, cols2_high[modes:], (((0,), (1,)), ((), ())), preferred_element_type=F32
        )

        pull = grads[pl.ds(here, 1), :] - jnp.sum(lam * pred_mean[0], axis=0, keepdims=True)
        mean_v = pred_mean[0] + jnp.sum(c_vv * pull, axis=1, keepdims=True)
        mean_r = pred_mean[1] + jnp.sum(c_rv * pull, axis=1, keepdims=True)
        means[pl.ds(here, 1), :] = diagonal(mean_v)
        diagonals[pl.ds(here, 1), :] = jnp.concatenate([diagonal(c_vv), diagonal(c_rr)], axis=1)
        rest4_f32 = rest4.astype(F32)
        bounds[pl.ds(jnp.minimum(step, 1), 1), :] = jnp.maximum(
            bounds[pl.ds(jnp.minimum(step, 1), 1), :], jnp.sum(rest4_f32 * rest4_f32, axis=0, keepdims=True)
        )

        a, b, c, d = columns[0], columns[1], columns[2], columns[3]
        pred_mean[0] = a * mean_v + b * mean_r
        pred_mean[1] = c * mean_v + d * mean_r
        g_vv = a * c_vv + b * c_rv
        g_vr = a * c_vr + b * c_rr
        g_rv = c * c_vv + d * c_rv
        g_rr = c * c_vr + d * c_rr
        p_vv[...] = g_vv * coef(0) + g_vr * coef(1) + eye * coef(4)
        p_rv[...] = g_rv * coef(0) + g_rr * coef(1) + eye * coef(5)
        p_vr[...] = g_vv * coef(2) + g_vr * coef(3) + eye * coef(5)
        p_rr[...] = g_rv * coef(2) + g_rr * coef(3) + eye * coef(6)
        gram_finish(total)
        return carry

    lax.fori_loop(0, steps, one_step, 0)

    m_high, m_low = split(means[...])
    m_split = jnp.concatenate(
        [jnp.concatenate([m_high, m_high], axis=1), jnp.concatenate([m_low, m_low], axis=1)], axis=0
    )
    f_both = dot(m_split, scaled_t_ref[...])
    scaled_field = f_both[:steps] + f_both[steps:]
    field_ref[...] = scaled_field[:local] * (root_ref[...] * noise_ref[...])
    variances_ref[...] = diagonals[:local, :]
    gap = readings[...] - mask_rows[...] * scaled_field
    squares = gap * gap
    row_sums[...] = jnp.sum(squares.reshape(steps, sensors // LANES, LANES), axis=1)

    def add_row(step, total):
        return total + row_sums[pl.ds(slot(step), 1), :]

    lane_total = lax.fori_loop(0, steps, add_row, jnp.zeros((1, LANES), F32))
    misfit_ref[...] = jnp.sum(lane_total, axis=1, keepdims=True) / (steps * sensors)
    worst_first = jnp.sum(bounds[0:1], axis=1, keepdims=True) / (LIMIT_FIRST * LIMIT_FIRST)
    worst_later = jnp.sum(bounds[1:2], axis=1, keepdims=True) / (LIMIT_LATER * LIMIT_LATER)
    bound_ref[...] = jnp.maximum(worst_first, worst_later)


def matmul(left, right):
    return jnp.dot(left, right, precision=lax.Precision.HIGHEST, preferred_element_type=F32)


def careful(order, local, blocks, arrived, block_of_sensor, sensor_basis, noise_var, mode_rate, mode_var):
    sensors, modes = sensor_basis.shape
    chunks = sensors // LANES
    in_time = arrived[order]
    observations = in_time[:, :chunks, :].reshape(-1, sensors)
    block_mask = in_time[:, chunks, :blocks]
    steps = observations.shape[0]
    f_vv, f_vr, f_rv, f_rr, root_value, root_cross, root_rate, sigma_vec = transition(mode_rate, mode_var)
    zero = jnp.zeros((modes, modes), F32)
    trans_mat = jnp.block([[jnp.diag(f_vv), jnp.diag(f_vr)], [jnp.diag(f_rv), jnp.diag(f_rr)]])
    lower_mat = jnp.block([[jnp.diag(root_value), zero], [jnp.diag(root_cross), jnp.diag(root_rate)]])
    noise_mat = matmul(lower_mat, lower_mat.T)
    stationary = jnp.diag(jnp.concatenate([sigma_vec * sigma_vec, sigma_vec * sigma_vec]))
    onehot = (block_of_sensor[:, None] == jnp.arange(blocks, dtype=jnp.int32)[None, :]).astype(F32)
    weights = matmul(block_mask, onehot.T) / noise_var[None, :]

    def one_step(carry, inputs):
        mean_vec, covar = carry
        weight_row, reading_row, step = inputs
        info_mat = matmul(sensor_basis.T * weight_row[None, :], sensor_basis)
        grad_vec = matmul((weight_row * reading_row)[None, :], sensor_basis)[0]
        trans_eff = jnp.where(step == 0, 0.0, trans_mat)
        noise_eff = jnp.where(step == 0, stationary, noise_mat)
        pred_mean = matmul(trans_eff, mean_vec[:, None])[:, 0]
        pred_cov = matmul(matmul(trans_eff, covar), trans_eff.T) + noise_eff
        factor_p = jnp.linalg.cholesky(pred_cov)
        top_rows = factor_p[:modes]
        inner = jnp.eye(2 * modes, dtype=F32) + matmul(matmul(top_rows.T, info_mat), top_rows)
        factor_m = jnp.linalg.cholesky(inner)
        solved = jax.scipy.linalg.solve_triangular(factor_m, factor_p.T, lower=True)
        new_cov = matmul(solved.T, solved)
        pull = grad_vec - matmul(info_mat, pred_mean[:modes, None])[:, 0]
        new_mean = pred_mean + matmul(new_cov[:, :modes], pull[:, None])[:, 0]
        return ((new_mean, new_cov), (new_mean, jnp.diagonal(new_cov)))

    start = (jnp.zeros((2 * modes,), F32), jnp.zeros((2 * modes, 2 * modes), F32))
    step_ids = jnp.arange(steps, dtype=jnp.int32)
    _, (means, variances) = lax.scan(one_step, start, (weights, observations, step_ids))
    field = matmul(means[:, :modes], sensor_basis.T)
    misfit = jnp.sum(weights * (observations - field) ** 2) / (steps * sensors)
    own = lax.axis_index(AXIS) * local
    own_field = lax.dynamic_slice_in_dim(field, own, local, 0)
    own_variances = lax.dynamic_slice_in_dim(variances, own, local, 0)
    return (own_field, own_variances, misfit.reshape(1, 1))


def in_vmem(count):
    return [pl.BlockSpec(memory_space=pltpu.VMEM)] * count


def on_device(observations, block_mask, block_of_sensor, sensor_basis, noise_var, mode_rate, mode_var):
    local, sensors = observations.shape
    modes = sensor_basis.shape[1]
    blocks = block_mask.shape[1]
    count = lax.axis_size(AXIS)
    steps = count * local
    noise_row = noise_var.reshape(1, sensors)
    position = lax.axis_index(AXIS).astype(jnp.int32)

    prepare = pl.pallas_call(
        prepare_kernel,
        out_shape=(
            jax.ShapeDtypeStruct((2 * modes, sensors), BF16),
            jax.ShapeDtypeStruct((sensors, 2 * modes), BF16),
            jax.ShapeDtypeStruct((blocks, sensors), BF16),
            jax.ShapeDtypeStruct((8, modes), F32),
        ),
        in_specs=[pl.BlockSpec(memory_space=pl.ANY)] + in_vmem(3),
        out_specs=tuple(in_vmem(4)),
        scratch_shapes=[pltpu.VMEM((sensors, modes), F32), pltpu.SemaphoreType.DMA((COPIES,))],
        compiler_params=pltpu.CompilerParams(vmem_limit_bytes=44 * 2**20),
        cost_estimate=pl.CostEstimate(flops=2 * sensors * modes, bytes_accessed=12 * sensors * modes, transcendentals=sensors),
        name="prepare",
    )
    block_row = block_of_sensor.reshape(1, sensors)
    rate_row = mode_rate.reshape(1, modes)
    var_row = mode_var.reshape(1, modes)

    pieces, prepared = exchange(
        observations,
        block_mask,
        count,
        lambda noise: sensor_basis * lax.rsqrt(noise)[:, None],
        lambda scaled: prepare(scaled, block_row, rate_row, var_row),
        noise_var,
    )
    scaled_t, scaled, onehot, coefs = prepared

    square = pltpu.VMEM((modes, modes), F32)
    field, variances, misfit, bound = pl.pallas_call(
        functools.partial(filter_kernel, count=count, local=local, blocks=blocks, parts=len(pieces)),
        out_shape=(
            jax.ShapeDtypeStruct((local, sensors), F32),
            jax.ShapeDtypeStruct((local, 2 * modes), F32),
            jax.ShapeDtypeStruct((1, 1), F32),
            jax.ShapeDtypeStruct((1, 1), F32),
        ),
        in_specs=[pl.BlockSpec(memory_space=pltpu.SMEM)] + in_vmem(len(pieces) + 5),
        out_specs=tuple(in_vmem(4)),
        scratch_shapes=[
            square,
            square,
            square,
            square,
            pltpu.VMEM((2, modes, modes), F32),
            pltpu.VMEM((4, modes, modes), F32),
            square,
            pltpu.VMEM((1, sensors), F32),
            pltpu.VMEM((steps, sensors), F32),
            pltpu.VMEM((steps, sensors), F32),
            pltpu.VMEM((steps, modes), F32),
            pltpu.VMEM((steps, modes), F32),
            pltpu.VMEM((steps, 2 * modes), F32),
            pltpu.VMEM((8, modes), F32),
            pltpu.VMEM((steps, LANES), F32),
        ],
        compiler_params=pltpu.CompilerParams(vmem_limit_bytes=20 * 2**20),
        cost_estimate=pl.CostEstimate(flops=steps * sensors * modes * 512, bytes_accessed=8 * sensors * modes, transcendentals=0),
        name="filter",
    )(position.reshape(1), *pieces, onehot, scaled_t, scaled, noise_row, coefs)

    step_ids = jnp.arange(steps, dtype=jnp.int32)
    order = slot_of((step_ids // local) ^ position, count, local) + step_ids % local
    field, variances, misfit = lax.cond(
        bound[0, 0] <= 1.0,
        lambda: (field, variances, misfit),
        lambda: careful(order, local, blocks, jnp.concatenate(pieces, axis=0), block_of_sensor, sensor_basis, noise_var, mode_rate, mode_var),
    )
    return (field, variances, misfit.reshape(1))


def solution(mesh):
    in_specs = (P(("groups", "tm"), None), P(("groups", "tm"), None), P(), P(), P(), P(), P())
    out_specs = (P(("groups", "tm"), None), P(("groups", "tm"), None), P("groups"))
    return jax.shard_map(on_device, mesh=mesh, in_specs=in_specs, out_specs=out_specs, check_vma=False)
```

```python
import functools

import jax
import jax.numpy as jnp
from jax import lax
from jax.experimental import pallas as pl
from jax.experimental.pallas import tpu as pltpu
from jax.sharding import PartitionSpec as P

BF16 = jnp.bfloat16
F32 = jnp.float32
AXIS = "tm"
LANES = 128
PIECES = 8
COPIES = 8
LIMIT_FIRST = 1.0e-2
LIMIT_LATER = 1.5e-3
PIVOT_FLOOR = 1.0e-6


def gather_rounds(count):
    bits = count.bit_length() - 1
    rounds = []
    top = bits
    if bits > 1 and (bits - 1) % 2 == 1:
        rounds.append((bits - 1, 1))
        top = bits - 1
    while top > 1:
        rounds.append((top - 2, 2))
        top -= 2
    if bits > 0:
        rounds.append((0, 1))
    return rounds


def swap(array, flip, count):
    return lax.ppermute(array, AXIS, [(p, p ^ flip) for p in range(count)])


def pack(observations, block_mask):
    local, sensors = observations.shape
    mask_row = jnp.pad(block_mask.astype(F32), ((0, 0), (0, LANES - block_mask.shape[1])))
    mask_tile = jnp.pad(mask_row.reshape(local, 1, LANES), ((0, 0), (0, 7), (0, 0)))
    return jnp.concatenate([observations.reshape(local, sensors // LANES, LANES), mask_tile], axis=1)


def exchange(observations, block_mask, count, early, late, seed):
    rounds = gather_rounds(count)
    pieces = [pack(observations, block_mask)]
    done = None
    for turn, (shift, width) in enumerate(rounds):
        flips = [digit << shift for digit in range(1, 1 << width)]
        rows = pieces[0] if turn == 0 else jnp.concatenate(pieces, axis=0)
        if turn == len(rounds) - 2:
            rows, seed = lax.optimization_barrier((rows, seed))
            seed = early(seed)
        if turn == len(rounds) - 1:
            rows, seed = lax.optimization_barrier((rows, seed))
            done = late(seed)
        if turn == 0:
            pieces = [rows] + [pack(swap(observations, flip, count), swap(block_mask, flip, count)) for flip in flips]
        else:
            pieces = [rows] + [swap(rows, flip, count) for flip in flips]
    return pieces, done


def slot_of(offset, count, local):
    slot = 0
    stride = local
    for shift, width in gather_rounds(count):
        slot = slot + ((offset >> shift) & ((1 << width) - 1)) * stride
        stride = stride << width
    return slot


def transition(mode_rate, mode_var):
    doubled = 2.0 * mode_rate
    damping = jnp.exp(-doubled)
    term_now = doubled * doubled * doubled / 6.0
    series = term_now
    for order in range(4, 15):
        term_now = term_now * doubled / order
        series = series + term_now
    q_value = mode_var * damping * series
    q_rate = mode_var * damping * (2.0 * doubled + series)
    q_cross = mode_var * damping * 2.0 * mode_rate * mode_rate
    root_value = jnp.sqrt(q_value)
    root_cross = q_cross / root_value
    root_rate = jnp.sqrt(q_value * q_rate - q_cross * q_cross) / root_value
    decay = jnp.exp(-mode_rate)
    return (
        decay * (1.0 + mode_rate),
        decay * mode_rate,
        -decay * mode_rate,
        decay * (1.0 - mode_rate),
        root_value,
        root_cross,
        root_rate,
        jnp.sqrt(mode_var),
    )


def split(x):
    high = x.astype(BF16)
    return high, (x - high.astype(F32)).astype(BF16)


def wide(x):
    return jnp.concatenate(split(x), axis=1)


def twice(x):
    return jnp.concatenate([x, x], axis=0)


def dot(left, right):
    return jnp.dot(left, right, preferred_element_type=F32)


def dot_split(left_wide, right_twice):
    both = dot(left_wide, right_twice)
    half = both.shape[1] // 2
    return both[:, :half] + both[:, half:]


def dot_three(left_wide, right):
    high, low = split(right)
    return dot(left_wide, twice(high)) + dot(left_wide[:, : high.shape[0]], low)


def prepare_kernel(
    basis_ref,
    block_ref,
    rate_ref,
    var_ref,
    scaled_t_ref,
    scaled_ref,
    onehot_ref,
    coef_ref,
    basis,
    arrivals,
):
    sensors, modes = basis_ref.shape
    depth = sensors // COPIES
    copies = []
    for part in range(COPIES):
        rows = pl.ds(part * depth, depth)
        copies.append(pltpu.make_async_copy(basis_ref.at[rows], basis.at[rows], arrivals.at[part]))
        copies[part].start()
    f_vv, f_vr, f_rv, f_rr, root_value, root_cross, root_rate, sigma_vec = transition(rate_ref[...], var_ref[...])
    rows = (
        f_vv,
        f_vr,
        f_rv,
        f_rr,
        root_value * root_value,
        root_value * root_cross,
        root_cross * root_cross + root_rate * root_rate,
        sigma_vec * sigma_vec,
    )
    coef_ref[...] = jnp.concatenate(rows, axis=0)
    block_index = lax.broadcasted_iota(jnp.int32, onehot_ref.shape, 0)
    onehot_ref[...] = jnp.where(block_index == block_ref[...], 1.0, 0.0).astype(BF16)
    for start in range(0, sensors, LANES):
        if start % depth == 0:
            copies[start // depth].wait()
        span = slice(start, start + LANES)
        chunk = basis[span, :]
        high, low = split(chunk.T)
        scaled_t_ref[:modes, span] = high
        scaled_t_ref[modes:, span] = low
        scaled_ref[span, :] = wide(chunk)


def filter_kernel(position_ref, *refs, count, local, blocks, parts):
    pieces = refs[:parts]
    (
        onehot_ref,
        scaled_t_ref,
        scaled_ref,
        noise_ref,
        coef_ref,
        field_ref,
        variances_ref,
        misfit_ref,
        p_vv,
        p_vr,
        p_rv,
        p_rr,
        pred_mean,
        columns,
        lam_now,
        root_ref,
        mask_rows,
        readings,
        grads,
        means,
        diagonals,
        bounds,
        row_sums,
        covar,
        mean_row,
        rest_g,
    ) = refs[parts:]
    modes = scaled_t_ref.shape[0] // 2
    sensors = scaled_t_ref.shape[1]
    piece_rows = pieces[0].shape[0]
    steps = parts * piece_rows
    chunks = sensors // LANES
    position = position_ref[0]
    row_index = lax.broadcasted_iota(jnp.int32, (modes, modes), 0)
    col_index = lax.broadcasted_iota(jnp.int32, (modes, modes), 1)
    eye = jnp.where(row_index == col_index, 1.0, 0.0).astype(F32)

    def coef(k):
        return coef_ref[k : k + 1, :]

    def slot(step):
        return slot_of((step // local) ^ position, count, local) + step % local

    def diagonal(square):
        return jnp.sum(eye * square, axis=0, keepdims=True)

    root_ref[...] = lax.rsqrt(noise_ref[...])
    masks = jnp.concatenate([ref[:, chunks, :blocks] for ref in pieces], axis=0).astype(BF16)
    mask_rows[...] = dot(masks, onehot_ref[...])
    for chunk in range(chunks):
        span = slice(chunk * LANES, (chunk + 1) * LANES)
        rows = jnp.concatenate([ref[:, chunk, :] for ref in pieces], axis=0)
        readings[:, span] = mask_rows[:, span] * rows * root_ref[:, span]
    for k in range(4):
        columns[k] = jnp.broadcast_to(jnp.sum(eye * coef(k), axis=1, keepdims=True), (modes, modes))
    stationary = eye * coef(7)
    p_vv[...] = stationary
    p_rr[...] = stationary
    p_vr[...] = jnp.zeros((modes, modes), F32)
    p_rv[...] = jnp.zeros((modes, modes), F32)
    pred_mean[...] = jnp.zeros(pred_mean.shape, F32)
    bounds[...] = jnp.zeros(bounds.shape, F32)

    depth = sensors // PIECES

    def gram_piece(piece, at):
        span = slice(piece * depth, (piece + 1) * depth)
        left = scaled_t_ref[:modes, span] * mask_rows[pl.ds(at, 1), span].astype(BF16)
        return dot(left, scaled_ref[span, :])

    def gram_finish(total):
        cross = total[:, modes:]
        lam_now[...] = total[:, :modes] + cross + cross.T

    first_left = scaled_t_ref[:modes, :] * mask_rows[pl.ds(slot(0), 1), :].astype(BF16)
    y_high, y_low = split(readings[...])
    first = dot(jnp.concatenate([first_left, y_high, y_low], axis=0), scaled_ref[...])
    gram_finish(first[:modes])
    g_half = first[modes:, :modes] + first[modes:, modes:]
    grads[...] = g_half[:steps] + g_half[steps:]

    def one_step(step, carry):
        here = slot(step)
        ahead = slot(jnp.minimum(step + 1, steps - 1))
        lam = lam_now[...]
        pred_vv = p_vv[...]
        pred_rv = p_rv[...]
        pred_rr = p_rr[...]
        lam_wide = wide(lam)
        lam_p = dot_three(lam_wide, pred_vv)
        cross = dot_three(lam_wide, p_vr[...])
        total = gram_piece(0, ahead) + gram_piece(1, ahead)
        scale = 1.0 / (1.0 + diagonal(lam) * diagonal(pred_vv))
        rest = eye * (1.0 - scale) - lam_p * scale
        scaled_p = jnp.concatenate([pred_vv * scale, pred_rv * scale], axis=0)
        second = dot_split(wide(jnp.concatenate([rest, scaled_p], axis=0)), twice(wide(rest)))
        total = total + (gram_piece(2, ahead) + gram_piece(3, ahead))
        rest2 = second[:modes]
        cols1 = scaled_p + second[modes:]
        rest2_high = rest2.astype(BF16)
        cross_high, cross_low = split(cross)
        rest4 = dot(rest2_high, rest2_high).astype(BF16)
        rest2_cross = dot(rest2_high, cross_high)
        cols_add = dot(cols1.astype(BF16), rest2_high)
        total = total + (gram_piece(4, ahead) + gram_piece(5, ahead))
        cols2 = cols1 + cols_add
        cols2_high, cols2_low = split(cols2)
        cols3 = cols2 + dot(cols2_high, rest4)
        cross_wide = jnp.concatenate([cross_high, cross_low], axis=1)
        taken = dot_split(
            jnp.concatenate([cols2_high[modes:], cols2_low[modes:]], axis=1), twice(cross_wide)
        ) + dot(cols_add[modes:].astype(BF16), rest2_cross.astype(BF16))
        total = total + (gram_piece(6, ahead) + gram_piece(7, ahead))
        c_rr = pred_rr - taken
        c_vv = cols3[:modes]
        c_rv = cols3[modes:]
        c_vr = cols2[modes:].T + lax.dot_general(
            rest4, cols2_high[modes:], (((0,), (1,)), ((), ())), preferred_element_type=F32
        )

        pull = grads[pl.ds(here, 1), :] - jnp.sum(lam * pred_mean[0], axis=0, keepdims=True)
        mean_v = pred_mean[0] + jnp.sum(c_vv * pull, axis=1, keepdims=True)
        mean_r = pred_mean[1] + jnp.sum(c_rv * pull, axis=1, keepdims=True)
        means[pl.ds(here, 1), :] = diagonal(mean_v)
        diagonals[pl.ds(here, 1), :] = jnp.concatenate([diagonal(c_vv), diagonal(c_rr)], axis=1)
        rest4_f32 = rest4.astype(F32)
        bounds[pl.ds(jnp.minimum(step, 1), 1), :] = jnp.maximum(
            bounds[pl.ds(jnp.minimum(step, 1), 1), :], jnp.sum(rest4_f32 * rest4_f32, axis=0, keepdims=True)
        )

        a, b, c, d = columns[0], columns[1], columns[2], columns[3]
        pred_mean[0] = a * mean_v + b * mean_r
        pred_mean[1] = c * mean_v + d * mean_r
        g_vv = a * c_vv + b * c_rv
        g_vr = a * c_vr + b * c_rr
        g_rv = c * c_vv + d * c_rv
        g_rr = c * c_vr + d * c_rr
        p_vv[...] = g_vv * coef(0) + g_vr * coef(1) + eye * coef(4)
        p_rv[...] = g_rv * coef(0) + g_rr * coef(1) + eye * coef(5)
        p_vr[...] = g_vv * coef(2) + g_vr * coef(3) + eye * coef(5)
        p_rr[...] = g_rv * coef(2) + g_rr * coef(3) + eye * coef(6)
        gram_finish(total)
        return carry

    lax.fori_loop(0, steps, one_step, 0)

    def careful_step(step, carry):
        here = slot(step)
        total = gram_piece(0, here)
        for piece in range(1, PIECES):
            total = total + gram_piece(piece, here)
        gram_finish(total)
        low = scaled_t_ref[modes:, :] * mask_rows[pl.ds(here, 1), :].astype(BF16)
        lam_now[...] = lam_now[...] + dot(low, scaled_ref[:, modes:])
        floor = PIVOT_FLOOR * jnp.max(diagonal(lam_now[...]), axis=1, keepdims=True)
        rest_g[...] = grads[pl.ds(here, 1), :]

        def one_pivot(k, inner):
            lam = lam_now[...]
            lanes = lax.broadcasted_iota(jnp.int32, (1, modes), 1)
            pivots = diagonal(lam)
            pivot = jnp.max(pivots, axis=1, keepdims=True)
            place = jnp.min(jnp.where(pivots == pivot, lanes, modes), axis=1, keepdims=True)
            pick = jnp.where(lanes == place, 1.0, 0.0)
            used = pivot > floor
            inverse = jnp.where(used, 1.0 / jnp.where(used, pivot, 1.0), 0.0)
            lam_col = jnp.sum(lam * pick, axis=1, keepdims=True)
            lam_row = jnp.sum(lam * jnp.sum(eye * pick, axis=1, keepdims=True), axis=0, keepdims=True)
            seen_row = lam_row * inverse
            seen_col = lam_col * inverse
            c_row = jnp.sum(covar[:modes, :] * seen_col, axis=0, keepdims=True)
            c_col = jnp.sum(covar[:, :modes] * seen_row, axis=1, keepdims=True)
            spread = jnp.sum(c_row[:, :modes] * seen_row, axis=1, keepdims=True)
            gain = jnp.where(used, pivot, 0.0) / (1.0 + jnp.where(used, pivot, 0.0) * spread)
            reading = jnp.sum(rest_g[...] * pick, axis=1, keepdims=True) * inverse
            surprise = reading - jnp.sum(mean_row[:, :modes] * seen_row, axis=1, keepdims=True)
            mean_row[...] = mean_row[...] + c_row * (gain * surprise)
            covar[...] = covar[...] - c_col * (c_row * gain)
            rest_g[...] = rest_g[...] - lam_row * reading
            lam_now[...] = lam - lam_col * seen_row
            return inner

        lax.fori_loop(0, modes, one_pivot, 0)
        c_vv = covar[:modes, :modes]
        c_vr = covar[:modes, modes:]
        c_rv = covar[modes:, :modes]
        c_rr = covar[modes:, modes:]
        mean_v = mean_row[:, :modes]
        mean_r = mean_row[:, modes:]
        means[pl.ds(here, 1), :] = mean_v
        diagonals[pl.ds(here, 1), :] = jnp.concatenate([diagonal(c_vv), diagonal(c_rr)], axis=1)
        mean_row[...] = jnp.concatenate([coef(0) * mean_v + coef(1) * mean_r, coef(2) * mean_v + coef(3) * mean_r], axis=1)
        a, b, c, d = columns[0], columns[1], columns[2], columns[3]
        g_vv = a * c_vv + b * c_rv
        g_vr = a * c_vr + b * c_rr
        g_rv = c * c_vv + d * c_rv
        g_rr = c * c_vr + d * c_rr
        covar[:modes, :modes] = g_vv * coef(0) + g_vr * coef(1) + eye * coef(4)
        covar[:modes, modes:] = g_vv * coef(2) + g_vr * coef(3) + eye * coef(5)
        covar[modes:, :modes] = g_rv * coef(0) + g_rr * coef(1) + eye * coef(5)
        covar[modes:, modes:] = g_rv * coef(2) + g_rr * coef(3) + eye * coef(6)
        return carry

    limits = jnp.where(lax.broadcasted_iota(jnp.int32, bounds.shape, 0) == 0, LIMIT_FIRST**-2.0, LIMIT_LATER**-2.0)
    settled = jnp.max(jnp.sum(bounds[...] * limits, axis=1, keepdims=True)) <= 1.0

    @pl.when(jnp.logical_not(settled))
    def _():
        covar[...] = jnp.zeros(covar.shape, F32)
        covar[:modes, :modes] = eye * coef(7)
        covar[modes:, modes:] = eye * coef(7)
        mean_row[...] = jnp.zeros(mean_row.shape, F32)
        lax.fori_loop(0, steps, careful_step, 0)

    m_high, m_low = split(means[...])
    m_split = jnp.concatenate(
        [jnp.concatenate([m_high, m_high], axis=1), jnp.concatenate([m_low, m_low], axis=1)], axis=0
    )
    f_both = dot(m_split, scaled_t_ref[...])
    scaled_field = f_both[:steps] + f_both[steps:]
    field_ref[...] = scaled_field[:local] * (root_ref[...] * noise_ref[...])
    variances_ref[...] = diagonals[:local, :]
    gap = readings[...] - mask_rows[...] * scaled_field
    squares = gap * gap
    row_sums[...] = jnp.sum(squares.reshape(steps, sensors // LANES, LANES), axis=1)

    def add_row(step, total):
        return total + row_sums[pl.ds(slot(step), 1), :]

    lane_total = lax.fori_loop(0, steps, add_row, jnp.zeros((1, LANES), F32))
    misfit_ref[...] = jnp.sum(lane_total, axis=1, keepdims=True) / (steps * sensors)


def in_vmem(count):
    return [pl.BlockSpec(memory_space=pltpu.VMEM)] * count


def on_device(observations, block_mask, block_of_sensor, sensor_basis, noise_var, mode_rate, mode_var):
    local, sensors = observations.shape
    modes = sensor_basis.shape[1]
    blocks = block_mask.shape[1]
    count = lax.axis_size(AXIS)
    steps = count * local
    noise_row = noise_var.reshape(1, sensors)
    position = lax.axis_index(AXIS).astype(jnp.int32)

    prepare = pl.pallas_call(
        prepare_kernel,
        out_shape=(
            jax.ShapeDtypeStruct((2 * modes, sensors), BF16),
            jax.ShapeDtypeStruct((sensors, 2 * modes), BF16),
            jax.ShapeDtypeStruct((blocks, sensors), BF16),
            jax.ShapeDtypeStruct((8, modes), F32),
        ),
        in_specs=[pl.BlockSpec(memory_space=pl.ANY)] + in_vmem(3),
        out_specs=tuple(in_vmem(4)),
        scratch_shapes=[pltpu.VMEM((sensors, modes), F32), pltpu.SemaphoreType.DMA((COPIES,))],
        compiler_params=pltpu.CompilerParams(vmem_limit_bytes=44 * 2**20),
        cost_estimate=pl.CostEstimate(flops=2 * sensors * modes, bytes_accessed=12 * sensors * modes, transcendentals=sensors),
        name="prepare",
    )
    block_row = block_of_sensor.reshape(1, sensors)
    rate_row = mode_rate.reshape(1, modes)
    var_row = mode_var.reshape(1, modes)

    pieces, prepared = exchange(
        observations,
        block_mask,
        count,
        lambda noise: sensor_basis * lax.rsqrt(noise)[:, None],
        lambda scaled: prepare(scaled, block_row, rate_row, var_row),
        noise_var,
    )
    scaled_t, scaled, onehot, coefs = prepared

    square = pltpu.VMEM((modes, modes), F32)
    field, variances, misfit = pl.pallas_call(
        functools.partial(filter_kernel, count=count, local=local, blocks=blocks, parts=len(pieces)),
        out_shape=(
            jax.ShapeDtypeStruct((local, sensors), F32),
            jax.ShapeDtypeStruct((local, 2 * modes), F32),
            jax.ShapeDtypeStruct((1, 1), F32),
        ),
        in_specs=[pl.BlockSpec(memory_space=pltpu.SMEM)] + in_vmem(len(pieces) + 5),
        out_specs=tuple(in_vmem(3)),
        scratch_shapes=[
            square,
            square,
            square,
            square,
            pltpu.VMEM((2, modes, modes), F32),
            pltpu.VMEM((4, modes, modes), F32),
            square,
            pltpu.VMEM((1, sensors), F32),
            pltpu.VMEM((steps, sensors), F32),
            pltpu.VMEM((steps, sensors), F32),
            pltpu.VMEM((steps, modes), F32),
            pltpu.VMEM((steps, modes), F32),
            pltpu.VMEM((steps, 2 * modes), F32),
            pltpu.VMEM((8, modes), F32),
            pltpu.VMEM((steps, LANES), F32),
            pltpu.VMEM((2 * modes, 2 * modes), F32),
            pltpu.VMEM((1, 2 * modes), F32),
            pltpu.VMEM((1, modes), F32),
        ],
        compiler_params=pltpu.CompilerParams(vmem_limit_bytes=20 * 2**20),
        cost_estimate=pl.CostEstimate(flops=steps * sensors * modes * 512, bytes_accessed=8 * sensors * modes, transcendentals=0),
        name="filter",
    )(position.reshape(1), *pieces, onehot, scaled_t, scaled, noise_row, coefs)

    return (field, variances, misfit.reshape(1))


def solution(mesh):
    in_specs = (P(("groups", "tm"), None), P(("groups", "tm"), None), P(), P(), P(), P(), P())
    out_specs = (P(("groups", "tm"), None), P(("groups", "tm"), None), P("groups"))
    return jax.shard_map(on_device, mesh=mesh, in_specs=in_specs, out_specs=out_specs, check_vma=False)
```

```python
import functools

import jax
import jax.numpy as jnp
from jax import lax
from jax.experimental import pallas as pl
from jax.experimental.pallas import tpu as pltpu
from jax.sharding import PartitionSpec as P

BF16 = jnp.bfloat16
F32 = jnp.float32
AXIS = "tm"
LANES = 128
PIECES = 8
COPIES = 8
LIMIT_FIRST = 1.0e-2
LIMIT_LATER = 1.5e-3
PIVOT_FLOOR = 1.0e-6


def gather_rounds(count):
    bits = count.bit_length() - 1
    rounds = []
    top = bits
    if bits > 1 and (bits - 1) % 2 == 1:
        rounds.append((bits - 1, 1))
        top = bits - 1
    while top > 1:
        rounds.append((top - 2, 2))
        top -= 2
    if bits > 0:
        rounds.append((0, 1))
    return rounds


def swap(array, flip, count):
    return lax.ppermute(array, AXIS, [(p, p ^ flip) for p in range(count)])


def pack(observations, block_mask):
    local, sensors = observations.shape
    mask_row = jnp.pad(block_mask.astype(F32), ((0, 0), (0, LANES - block_mask.shape[1])))
    mask_tile = jnp.pad(mask_row.reshape(local, 1, LANES), ((0, 0), (0, 7), (0, 0)))
    return jnp.concatenate([observations.reshape(local, sensors // LANES, LANES), mask_tile], axis=1)


def exchange(observations, block_mask, count, early, late, seed):
    rounds = gather_rounds(count)
    pieces = [pack(observations, block_mask)]
    done = None
    for turn, (shift, width) in enumerate(rounds):
        flips = [digit << shift for digit in range(1, 1 << width)]
        rows = pieces[0] if turn == 0 else jnp.concatenate(pieces, axis=0)
        if turn == len(rounds) - 2:
            rows, seed = lax.optimization_barrier((rows, seed))
            seed = early(seed)
        if turn == len(rounds) - 1:
            rows, seed = lax.optimization_barrier((rows, seed))
            done = late(seed)
        if turn == 0:
            pieces = [rows] + [pack(swap(observations, flip, count), swap(block_mask, flip, count)) for flip in flips]
        else:
            pieces = [rows] + [swap(rows, flip, count) for flip in flips]
    return pieces, done


def slot_of(offset, count, local):
    slot = 0
    stride = local
    for shift, width in gather_rounds(count):
        slot = slot + ((offset >> shift) & ((1 << width) - 1)) * stride
        stride = stride << width
    return slot


def transition(mode_rate, mode_var):
    doubled = 2.0 * mode_rate
    damping = jnp.exp(-doubled)
    term_now = doubled * doubled * doubled / 6.0
    series = term_now
    for order in range(4, 15):
        term_now = term_now * doubled / order
        series = series + term_now
    q_value = mode_var * damping * series
    q_rate = mode_var * damping * (2.0 * doubled + series)
    q_cross = mode_var * damping * 2.0 * mode_rate * mode_rate
    root_value = jnp.sqrt(q_value)
    root_cross = q_cross / root_value
    root_rate = jnp.sqrt(q_value * q_rate - q_cross * q_cross) / root_value
    decay = jnp.exp(-mode_rate)
    return (
        decay * (1.0 + mode_rate),
        decay * mode_rate,
        -decay * mode_rate,
        decay * (1.0 - mode_rate),
        root_value,
        root_cross,
        root_rate,
        jnp.sqrt(mode_var),
    )


def split(x):
    high = x.astype(BF16)
    return high, (x - high.astype(F32)).astype(BF16)


def wide(x):
    return jnp.concatenate(split(x), axis=1)


def twice(x):
    return jnp.concatenate([x, x], axis=0)


def dot(left, right):
    return jnp.dot(left, right, preferred_element_type=F32)


def dot_split(left_wide, right_twice):
    both = dot(left_wide, right_twice)
    half = both.shape[1] // 2
    return both[:, :half] + both[:, half:]


def dot_three(left_wide, right):
    high, low = split(right)
    return dot(left_wide, twice(high)) + dot(left_wide[:, : high.shape[0]], low)


def prepare_kernel(
    basis_ref,
    block_ref,
    rate_ref,
    var_ref,
    scaled_t_ref,
    scaled_ref,
    onehot_ref,
    coef_ref,
    basis,
    arrivals,
):
    sensors, modes = basis_ref.shape
    depth = sensors // COPIES
    copies = []
    for part in range(COPIES):
        rows = pl.ds(part * depth, depth)
        copies.append(pltpu.make_async_copy(basis_ref.at[rows], basis.at[rows], arrivals.at[part]))
        copies[part].start()
    f_vv, f_vr, f_rv, f_rr, root_value, root_cross, root_rate, sigma_vec = transition(rate_ref[...], var_ref[...])
    rows = (
        f_vv,
        f_vr,
        f_rv,
        f_rr,
        root_value * root_value,
        root_value * root_cross,
        root_cross * root_cross + root_rate * root_rate,
        sigma_vec * sigma_vec,
    )
    coef_ref[...] = jnp.concatenate(rows, axis=0)
    block_index = lax.broadcasted_iota(jnp.int32, onehot_ref.shape, 0)
    onehot_ref[...] = jnp.where(block_index == block_ref[...], 1.0, 0.0).astype(BF16)
    for start in range(0, sensors, LANES):
        if start % depth == 0:
            copies[start // depth].wait()
        span = slice(start, start + LANES)
        chunk = basis[span, :]
        high, low = split(chunk.T)
        scaled_t_ref[:modes, span] = high
        scaled_t_ref[modes:, span] = low
        scaled_ref[span, :] = wide(chunk)


def filter_kernel(position_ref, *refs, count, local, blocks, parts):
    pieces = refs[:parts]
    (
        onehot_ref,
        scaled_t_ref,
        scaled_ref,
        noise_ref,
        coef_ref,
        field_ref,
        variances_ref,
        misfit_ref,
        p_vv,
        p_vr,
        p_rv,
        p_rr,
        pred_mean,
        columns,
        lam_now,
        root_ref,
        mask_rows,
        readings,
        grads,
        means,
        diagonals,
        bounds,
        row_sums,
        covar,
        mean_row,
        rest_g,
    ) = refs[parts:]
    modes = scaled_t_ref.shape[0] // 2
    sensors = scaled_t_ref.shape[1]
    piece_rows = pieces[0].shape[0]
    steps = parts * piece_rows
    chunks = sensors // LANES
    position = position_ref[0]
    row_index = lax.broadcasted_iota(jnp.int32, (modes, modes), 0)
    col_index = lax.broadcasted_iota(jnp.int32, (modes, modes), 1)
    eye = jnp.where(row_index == col_index, 1.0, 0.0).astype(F32)

    def coef(k):
        return coef_ref[k : k + 1, :]

    def slot(step):
        return slot_of((step // local) ^ position, count, local) + step % local

    def diagonal(square):
        return jnp.sum(eye * square, axis=0, keepdims=True)

    root_ref[...] = lax.rsqrt(noise_ref[...])
    masks = jnp.concatenate([ref[:, chunks, :blocks] for ref in pieces], axis=0).astype(BF16)
    mask_rows[...] = dot(masks, onehot_ref[...])
    for chunk in range(chunks):
        span = slice(chunk * LANES, (chunk + 1) * LANES)
        rows = jnp.concatenate([ref[:, chunk, :] for ref in pieces], axis=0)
        readings[:, span] = mask_rows[:, span] * rows * root_ref[:, span]
    for k in range(4):
        columns[k] = jnp.broadcast_to(jnp.sum(eye * coef(k), axis=1, keepdims=True), (modes, modes))
    stationary = eye * coef(7)
    p_vv[...] = stationary
    p_rr[...] = stationary
    p_vr[...] = jnp.zeros((modes, modes), F32)
    p_rv[...] = jnp.zeros((modes, modes), F32)
    pred_mean[...] = jnp.zeros(pred_mean.shape, F32)
    bounds[...] = jnp.zeros(bounds.shape, F32)

    depth = sensors // PIECES

    def gram_piece(piece, at):
        span = slice(piece * depth, (piece + 1) * depth)
        left = scaled_t_ref[:modes, span] * mask_rows[pl.ds(at, 1), span].astype(BF16)
        return dot(left, scaled_ref[span, :])

    def gram_finish(total):
        cross = total[:, modes:]
        lam_now[...] = total[:, :modes] + cross + cross.T

    first_left = scaled_t_ref[:modes, :] * mask_rows[pl.ds(slot(0), 1), :].astype(BF16)
    y_high, y_low = split(readings[...])
    first = dot(jnp.concatenate([first_left, y_high, y_low], axis=0), scaled_ref[...])
    gram_finish(first[:modes])
    g_half = first[modes:, :modes] + first[modes:, modes:]
    grads[...] = g_half[:steps] + g_half[steps:]

    def one_step(step, carry, last=False):
        here = slot(step)
        ahead = slot(step + 1)
        lam = lam_now[...]
        pred_vv = p_vv[...]
        pred_rv = p_rv[...]
        pred_rr = p_rr[...]
        lam_wide = wide(lam)
        lam_p = dot_three(lam_wide, pred_vv)
        cross = dot_three(lam_wide, p_vr[...])
        total = None if last else gram_piece(0, ahead) + gram_piece(1, ahead)
        scale = 1.0 / (1.0 + diagonal(lam) * diagonal(pred_vv))
        rest = eye * (1.0 - scale) - lam_p * scale
        scaled_p = jnp.concatenate([pred_vv * scale, pred_rv * scale], axis=0)
        second = dot_split(wide(jnp.concatenate([rest, scaled_p], axis=0)), twice(wide(rest)))
        if not last:
            total = total + (gram_piece(2, ahead) + gram_piece(3, ahead))
        rest2 = second[:modes]
        cols1 = scaled_p + second[modes:]
        rest2_high = rest2.astype(BF16)
        cross_high, cross_low = split(cross)
        rest4 = dot(rest2_high, rest2_high).astype(BF16)
        rest2_cross = dot(rest2_high, cross_high)
        cols_add = dot(cols1.astype(BF16), rest2_high)
        if not last:
            total = total + (gram_piece(4, ahead) + gram_piece(5, ahead))
        cols2 = cols1 + cols_add
        cols2_high, cols2_low = split(cols2)
        cols3 = cols2 + dot(cols2_high, rest4)
        cross_wide = jnp.concatenate([cross_high, cross_low], axis=1)
        taken = dot_split(
            jnp.concatenate([cols2_high[modes:], cols2_low[modes:]], axis=1), twice(cross_wide)
        ) + dot(cols_add[modes:].astype(BF16), rest2_cross.astype(BF16))
        if not last:
            total = total + (gram_piece(6, ahead) + gram_piece(7, ahead))
        c_rr = pred_rr - taken
        c_vv = cols3[:modes]
        c_rv = cols3[modes:]
        c_vr = cols2[modes:].T + lax.dot_general(
            rest4, cols2_high[modes:], (((0,), (1,)), ((), ())), preferred_element_type=F32
        )

        pull = grads[pl.ds(here, 1), :] - jnp.sum(lam * pred_mean[0], axis=0, keepdims=True)
        mean_v = pred_mean[0] + jnp.sum(c_vv * pull, axis=1, keepdims=True)
        mean_r = pred_mean[1] + jnp.sum(c_rv * pull, axis=1, keepdims=True)
        means[pl.ds(here, 1), :] = diagonal(mean_v)
        diagonals[pl.ds(here, 1), :] = jnp.concatenate([diagonal(c_vv), diagonal(c_rr)], axis=1)
        rest4_f32 = rest4.astype(F32)
        bounds[pl.ds(jnp.minimum(step, 1), 1), :] = jnp.maximum(
            bounds[pl.ds(jnp.minimum(step, 1), 1), :], jnp.sum(rest4_f32 * rest4_f32, axis=0, keepdims=True)
        )

        if last:
            return carry
        a, b, c, d = columns[0], columns[1], columns[2], columns[3]
        pred_mean[0] = a * mean_v + b * mean_r
        pred_mean[1] = c * mean_v + d * mean_r
        g_vv = a * c_vv + b * c_rv
        g_vr = a * c_vr + b * c_rr
        g_rv = c * c_vv + d * c_rv
        g_rr = c * c_vr + d * c_rr
        p_vv[...] = g_vv * coef(0) + g_vr * coef(1) + eye * coef(4)
        p_rv[...] = g_rv * coef(0) + g_rr * coef(1) + eye * coef(5)
        p_vr[...] = g_vv * coef(2) + g_vr * coef(3) + eye * coef(5)
        p_rr[...] = g_rv * coef(2) + g_rr * coef(3) + eye * coef(6)
        gram_finish(total)
        return carry

    lax.fori_loop(0, steps - 1, one_step, 0)
    one_step(steps - 1, 0, last=True)

    def careful_step(step, carry):
        here = slot(step)
        total = gram_piece(0, here)
        for piece in range(1, PIECES):
            total = total + gram_piece(piece, here)
        gram_finish(total)
        low = scaled_t_ref[modes:, :] * mask_rows[pl.ds(here, 1), :].astype(BF16)
        lam_now[...] = lam_now[...] + dot(low, scaled_ref[:, modes:])
        floor = PIVOT_FLOOR * jnp.max(diagonal(lam_now[...]), axis=1, keepdims=True)
        rest_g[...] = grads[pl.ds(here, 1), :]

        def one_pivot(k, inner):
            lam = lam_now[...]
            lanes = lax.broadcasted_iota(jnp.int32, (1, modes), 1)
            pivots = diagonal(lam)
            pivot = jnp.max(pivots, axis=1, keepdims=True)
            place = jnp.min(jnp.where(pivots == pivot, lanes, modes), axis=1, keepdims=True)
            pick = jnp.where(lanes == place, 1.0, 0.0)
            used = pivot > floor
            inverse = jnp.where(used, 1.0 / jnp.where(used, pivot, 1.0), 0.0)
            lam_col = jnp.sum(lam * pick, axis=1, keepdims=True)
            lam_row = jnp.sum(lam * jnp.sum(eye * pick, axis=1, keepdims=True), axis=0, keepdims=True)
            seen_row = lam_row * inverse
            seen_col = lam_col * inverse
            c_row = jnp.sum(covar[:modes, :] * seen_col, axis=0, keepdims=True)
            c_col = jnp.sum(covar[:, :modes] * seen_row, axis=1, keepdims=True)
            spread = jnp.sum(c_row[:, :modes] * seen_row, axis=1, keepdims=True)
            gain = jnp.where(used, pivot, 0.0) / (1.0 + jnp.where(used, pivot, 0.0) * spread)
            reading = jnp.sum(rest_g[...] * pick, axis=1, keepdims=True) * inverse
            surprise = reading - jnp.sum(mean_row[:, :modes] * seen_row, axis=1, keepdims=True)
            mean_row[...] = mean_row[...] + c_row * (gain * surprise)
            covar[...] = covar[...] - c_col * (c_row * gain)
            rest_g[...] = rest_g[...] - lam_row * reading
            lam_now[...] = lam - lam_col * seen_row
            return inner

        lax.fori_loop(0, modes, one_pivot, 0)
        c_vv = covar[:modes, :modes]
        c_vr = covar[:modes, modes:]
        c_rv = covar[modes:, :modes]
        c_rr = covar[modes:, modes:]
        mean_v = mean_row[:, :modes]
        mean_r = mean_row[:, modes:]
        means[pl.ds(here, 1), :] = mean_v
        diagonals[pl.ds(here, 1), :] = jnp.concatenate([diagonal(c_vv), diagonal(c_rr)], axis=1)
        mean_row[...] = jnp.concatenate([coef(0) * mean_v + coef(1) * mean_r, coef(2) * mean_v + coef(3) * mean_r], axis=1)
        a, b, c, d = columns[0], columns[1], columns[2], columns[3]
        g_vv = a * c_vv + b * c_rv
        g_vr = a * c_vr + b * c_rr
        g_rv = c * c_vv + d * c_rv
        g_rr = c * c_vr + d * c_rr
        covar[:modes, :modes] = g_vv * coef(0) + g_vr * coef(1) + eye * coef(4)
        covar[:modes, modes:] = g_vv * coef(2) + g_vr * coef(3) + eye * coef(5)
        covar[modes:, :modes] = g_rv * coef(0) + g_rr * coef(1) + eye * coef(5)
        covar[modes:, modes:] = g_rv * coef(2) + g_rr * coef(3) + eye * coef(6)
        return carry

    limits = jnp.where(lax.broadcasted_iota(jnp.int32, bounds.shape, 0) == 0, LIMIT_FIRST**-2.0, LIMIT_LATER**-2.0)
    settled = jnp.max(jnp.sum(bounds[...] * limits, axis=1, keepdims=True)) <= 1.0

    @pl.when(jnp.logical_not(settled))
    def _():
        covar[...] = jnp.zeros(covar.shape, F32)
        covar[:modes, :modes] = eye * coef(7)
        covar[modes:, modes:] = eye * coef(7)
        mean_row[...] = jnp.zeros(mean_row.shape, F32)
        lax.fori_loop(0, steps, careful_step, 0)

    m_high, m_low = split(means[...])
    m_split = jnp.concatenate(
        [jnp.concatenate([m_high, m_high], axis=1), jnp.concatenate([m_low, m_low], axis=1)], axis=0
    )
    f_both = dot(m_split, scaled_t_ref[...])
    scaled_field = f_both[:steps] + f_both[steps:]
    field_ref[...] = scaled_field[:local] * (root_ref[...] * noise_ref[...])
    variances_ref[...] = diagonals[:local, :]
    gap = readings[...] - mask_rows[...] * scaled_field
    squares = gap * gap
    lanes_first = squares[:, :LANES]
    for chunk in range(1, chunks):
        lanes_first = lanes_first + squares[:, chunk * LANES : (chunk + 1) * LANES]
    row_sums[...] = lanes_first
    lane_total = row_sums[pl.ds(slot(0), 1), :]
    for step in range(1, steps):
        lane_total = lane_total + row_sums[pl.ds(slot(step), 1), :]
    misfit_ref[...] = jnp.sum(lane_total, axis=1, keepdims=True) / (steps * sensors)


def in_vmem(count):
    return [pl.BlockSpec(memory_space=pltpu.VMEM)] * count


def on_device(observations, block_mask, block_of_sensor, sensor_basis, noise_var, mode_rate, mode_var):
    local, sensors = observations.shape
    modes = sensor_basis.shape[1]
    blocks = block_mask.shape[1]
    count = lax.axis_size(AXIS)
    steps = count * local
    noise_row = noise_var.reshape(1, sensors)
    position = lax.axis_index(AXIS).astype(jnp.int32)

    prepare = pl.pallas_call(
        prepare_kernel,
        out_shape=(
            jax.ShapeDtypeStruct((2 * modes, sensors), BF16),
            jax.ShapeDtypeStruct((sensors, 2 * modes), BF16),
            jax.ShapeDtypeStruct((blocks, sensors), BF16),
            jax.ShapeDtypeStruct((8, modes), F32),
        ),
        in_specs=[pl.BlockSpec(memory_space=pl.ANY)] + in_vmem(3),
        out_specs=tuple(in_vmem(4)),
        scratch_shapes=[pltpu.VMEM((sensors, modes), F32), pltpu.SemaphoreType.DMA((COPIES,))],
        compiler_params=pltpu.CompilerParams(vmem_limit_bytes=44 * 2**20),
        cost_estimate=pl.CostEstimate(flops=2 * sensors * modes, bytes_accessed=12 * sensors * modes, transcendentals=sensors),
        name="prepare",
    )
    block_row = block_of_sensor.reshape(1, sensors)
    rate_row = mode_rate.reshape(1, modes)
    var_row = mode_var.reshape(1, modes)

    pieces, prepared = exchange(
        observations,
        block_mask,
        count,
        lambda noise: sensor_basis * lax.rsqrt(noise)[:, None],
        lambda scaled: prepare(scaled, block_row, rate_row, var_row),
        noise_var,
    )
    scaled_t, scaled, onehot, coefs = prepared

    square = pltpu.VMEM((modes, modes), F32)
    field, variances, misfit = pl.pallas_call(
        functools.partial(filter_kernel, count=count, local=local, blocks=blocks, parts=len(pieces)),
        out_shape=(
            jax.ShapeDtypeStruct((local, sensors), F32),
            jax.ShapeDtypeStruct((local, 2 * modes), F32),
            jax.ShapeDtypeStruct((1, 1), F32),
        ),
        in_specs=[pl.BlockSpec(memory_space=pltpu.SMEM)] + in_vmem(len(pieces) + 5),
        out_specs=tuple(in_vmem(3)),
        scratch_shapes=[
            square,
            square,
            square,
            square,
            pltpu.VMEM((2, modes, modes), F32),
            pltpu.VMEM((4, modes, modes), F32),
            square,
            pltpu.VMEM((1, sensors), F32),
            pltpu.VMEM((steps, sensors), F32),
            pltpu.VMEM((steps, sensors), F32),
            pltpu.VMEM((steps, modes), F32),
            pltpu.VMEM((steps, modes), F32),
            pltpu.VMEM((steps, 2 * modes), F32),
            pltpu.VMEM((8, modes), F32),
            pltpu.VMEM((steps, LANES), F32),
            pltpu.VMEM((2 * modes, 2 * modes), F32),
            pltpu.VMEM((1, 2 * modes), F32),
            pltpu.VMEM((1, modes), F32),
        ],
        compiler_params=pltpu.CompilerParams(vmem_limit_bytes=20 * 2**20),
        cost_estimate=pl.CostEstimate(flops=steps * sensors * modes * 512, bytes_accessed=8 * sensors * modes, transcendentals=0),
        name="filter",
    )(position.reshape(1), *pieces, onehot, scaled_t, scaled, noise_row, coefs)

    return (field, variances, misfit.reshape(1))


def solution(mesh):
    in_specs = (P(("groups", "tm"), None), P(("groups", "tm"), None), P(), P(), P(), P(), P())
    out_specs = (P(("groups", "tm"), None), P(("groups", "tm"), None), P("groups"))
    return jax.shard_map(on_device, mesh=mesh, in_specs=in_specs, out_specs=out_specs, check_vma=False)
```

```python
import functools

import jax
import jax.numpy as jnp
from jax import lax
from jax.experimental import pallas as pl
from jax.experimental.pallas import tpu as pltpu
from jax.sharding import PartitionSpec as P

BF16 = jnp.bfloat16
F32 = jnp.float32
AXIS = "tm"
LANES = 128
PIECES = 8
COPIES = 4
LIMIT_FIRST = 1.0e-2
LIMIT_LATER = 1.5e-3
PIVOT_FLOOR = 1.0e-6


def gather_rounds(count):
    bits = count.bit_length() - 1
    rounds = []
    top = bits
    if bits > 1 and (bits - 1) % 2 == 1:
        rounds.append((bits - 1, 1))
        top = bits - 1
    while top > 1:
        rounds.append((top - 2, 2))
        top -= 2
    if bits > 0:
        rounds.append((0, 1))
    return rounds


def swap(array, flip, count):
    return lax.ppermute(array, AXIS, [(p, p ^ flip) for p in range(count)])


def pack(observations, block_mask):
    local, sensors = observations.shape
    mask_row = jnp.pad(block_mask.astype(F32), ((0, 0), (0, LANES - block_mask.shape[1])))
    mask_tile = jnp.pad(mask_row.reshape(local, 1, LANES), ((0, 0), (0, 7), (0, 0)))
    return jnp.concatenate([observations.reshape(local, sensors // LANES, LANES), mask_tile], axis=1)


def exchange(observations, block_mask, count, early, late, seed):
    rounds = gather_rounds(count)
    pieces = [pack(observations, block_mask)]
    done = None
    for turn, (shift, width) in enumerate(rounds):
        flips = [digit << shift for digit in range(1, 1 << width)]
        rows = pieces[0] if turn == 0 else jnp.concatenate(pieces, axis=0)
        if turn == len(rounds) - 2:
            rows, seed = lax.optimization_barrier((rows, seed))
            seed = early(seed)
        if turn == len(rounds) - 1:
            rows, seed = lax.optimization_barrier((rows, seed))
            done = late(seed)
        if turn == 0:
            pieces = [rows] + [pack(swap(observations, flip, count), swap(block_mask, flip, count)) for flip in flips]
        else:
            pieces = [rows] + [swap(rows, flip, count) for flip in flips]
    return pieces, done


def slot_of(offset, count, local):
    slot = 0
    stride = local
    for shift, width in gather_rounds(count):
        slot = slot + ((offset >> shift) & ((1 << width) - 1)) * stride
        stride = stride << width
    return slot


def transition(mode_rate, mode_var):
    doubled = 2.0 * mode_rate
    damping = jnp.exp(-doubled)
    term_now = doubled * doubled * doubled / 6.0
    series = term_now
    for order in range(4, 15):
        term_now = term_now * doubled / order
        series = series + term_now
    q_value = mode_var * damping * series
    q_rate = mode_var * damping * (2.0 * doubled + series)
    q_cross = mode_var * damping * 2.0 * mode_rate * mode_rate
    root_value = jnp.sqrt(q_value)
    root_cross = q_cross / root_value
    root_rate = jnp.sqrt(q_value * q_rate - q_cross * q_cross) / root_value
    decay = jnp.exp(-mode_rate)
    return (
        decay * (1.0 + mode_rate),
        decay * mode_rate,
        -decay * mode_rate,
        decay * (1.0 - mode_rate),
        root_value,
        root_cross,
        root_rate,
        jnp.sqrt(mode_var),
    )


def split(x):
    high = x.astype(BF16)
    return high, (x - high.astype(F32)).astype(BF16)


def wide(x):
    return jnp.concatenate(split(x), axis=1)


def twice(x):
    return jnp.concatenate([x, x], axis=0)


def dot(left, right):
    return jnp.dot(left, right, preferred_element_type=F32)


def dot_split(left_wide, right_twice):
    both = dot(left_wide, right_twice)
    half = both.shape[1] // 2
    return both[:, :half] + both[:, half:]


def dot_three(left_wide, right):
    high, low = split(right)
    return dot(left_wide, twice(high)) + dot(left_wide[:, : high.shape[0]], low)


def prepare_kernel(
    basis_ref,
    block_ref,
    rate_ref,
    var_ref,
    scaled_t_ref,
    scaled_ref,
    onehot_ref,
    coef_ref,
    basis,
    arrivals,
):
    sensors, modes = basis_ref.shape
    depth = sensors // COPIES
    copies = []
    for part in range(COPIES):
        rows = pl.ds(part * depth, depth)
        copies.append(pltpu.make_async_copy(basis_ref.at[rows], basis.at[rows], arrivals.at[part]))
        copies[part].start()
    f_vv, f_vr, f_rv, f_rr, root_value, root_cross, root_rate, sigma_vec = transition(rate_ref[...], var_ref[...])
    rows = (
        f_vv,
        f_vr,
        f_rv,
        f_rr,
        root_value * root_value,
        root_value * root_cross,
        root_cross * root_cross + root_rate * root_rate,
        sigma_vec * sigma_vec,
    )
    coef_ref[...] = jnp.concatenate(rows, axis=0)
    block_index = lax.broadcasted_iota(jnp.int32, onehot_ref.shape, 0)
    onehot_ref[...] = jnp.where(block_index == block_ref[...], 1.0, 0.0).astype(BF16)
    for start in range(0, sensors, LANES):
        if start % depth == 0:
            copies[start // depth].wait()
        span = slice(start, start + LANES)
        chunk = basis[span, :]
        high, low = split(chunk.T)
        scaled_t_ref[:modes, span] = high
        scaled_t_ref[modes:, span] = low
        scaled_ref[span, :] = wide(chunk)


def filter_kernel(position_ref, *refs, count, local, blocks, parts):
    pieces = refs[:parts]
    (
        onehot_ref,
        scaled_t_ref,
        scaled_ref,
        noise_ref,
        coef_ref,
        field_ref,
        variances_ref,
        misfit_ref,
        p_vv,
        p_vr,
        p_rv,
        p_rr,
        pred_mean,
        columns,
        lam_now,
        root_ref,
        mask_rows,
        readings,
        grads,
        means,
        diagonals,
        bounds,
        row_sums,
        covar,
        mean_row,
        rest_g,
    ) = refs[parts:]
    modes = scaled_t_ref.shape[0] // 2
    sensors = scaled_t_ref.shape[1]
    piece_rows = pieces[0].shape[0]
    steps = parts * piece_rows
    chunks = sensors // LANES
    position = position_ref[0]
    row_index = lax.broadcasted_iota(jnp.int32, (modes, modes), 0)
    col_index = lax.broadcasted_iota(jnp.int32, (modes, modes), 1)
    eye = jnp.where(row_index == col_index, 1.0, 0.0).astype(F32)

    def coef(k):
        return coef_ref[k : k + 1, :]

    def slot(step):
        return slot_of((step // local) ^ position, count, local) + step % local

    def diagonal(square):
        return jnp.sum(eye * square, axis=0, keepdims=True)

    root_ref[...] = lax.rsqrt(noise_ref[...])
    masks = jnp.concatenate([ref[:, chunks, :blocks] for ref in pieces], axis=0).astype(BF16)
    mask_rows[...] = dot(masks, onehot_ref[...])
    for chunk in range(chunks):
        span = slice(chunk * LANES, (chunk + 1) * LANES)
        rows = jnp.concatenate([ref[:, chunk, :] for ref in pieces], axis=0)
        readings[:, span] = mask_rows[:, span] * rows * root_ref[:, span]
    for k in range(4):
        columns[k] = jnp.broadcast_to(jnp.sum(eye * coef(k), axis=1, keepdims=True), (modes, modes))
    stationary = eye * coef(7)
    p_vv[...] = stationary
    p_rr[...] = stationary
    p_vr[...] = jnp.zeros((modes, modes), F32)
    p_rv[...] = jnp.zeros((modes, modes), F32)
    pred_mean[...] = jnp.zeros(pred_mean.shape, F32)
    bounds[...] = jnp.zeros(bounds.shape, F32)

    depth = sensors // PIECES

    def gram_piece(piece, at):
        span = slice(piece * depth, (piece + 1) * depth)
        left = scaled_t_ref[:modes, span] * mask_rows[pl.ds(at, 1), span].astype(BF16)
        return dot(left, scaled_ref[span, :])

    def gram_finish(total):
        cross = total[:, modes:]
        lam_now[...] = total[:, :modes] + cross + cross.T

    first_left = scaled_t_ref[:modes, :] * mask_rows[pl.ds(slot(0), 1), :].astype(BF16)
    y_high, y_low = split(readings[...])
    first = dot(jnp.concatenate([first_left, y_high, y_low], axis=0), scaled_ref[...])
    gram_finish(first[:modes])
    g_half = first[modes:, :modes] + first[modes:, modes:]
    grads[...] = g_half[:steps] + g_half[steps:]

    def one_step(step, carry, last=False):
        here = slot(step)
        ahead = slot(step + 1)
        lam = lam_now[...]
        pred_vv = p_vv[...]
        pred_rv = p_rv[...]
        pred_rr = p_rr[...]
        lam_wide = wide(lam)
        lam_p = dot_three(lam_wide, pred_vv)
        cross = dot_three(lam_wide, p_vr[...])
        total = None if last else gram_piece(0, ahead) + gram_piece(1, ahead)
        scale = 1.0 / (1.0 + diagonal(lam) * diagonal(pred_vv))
        rest = eye * (1.0 - scale) - lam_p * scale
        scaled_p = jnp.concatenate([pred_vv * scale, pred_rv * scale], axis=0)
        second = dot_split(wide(jnp.concatenate([rest, scaled_p], axis=0)), twice(wide(rest)))
        if not last:
            total = total + (gram_piece(2, ahead) + gram_piece(3, ahead))
        rest2 = second[:modes]
        cols1 = scaled_p + second[modes:]
        rest2_high = rest2.astype(BF16)
        cross_high, cross_low = split(cross)
        rest4 = dot(rest2_high, rest2_high).astype(BF16)
        rest2_cross = dot(rest2_high, cross_high)
        cols_add = dot(cols1.astype(BF16), rest2_high)
        if not last:
            total = total + (gram_piece(4, ahead) + gram_piece(5, ahead))
        cols2 = cols1 + cols_add
        cols2_high, cols2_low = split(cols2)
        cols3 = cols2 + dot(cols2_high, rest4)
        cross_wide = jnp.concatenate([cross_high, cross_low], axis=1)
        taken = dot_split(
            jnp.concatenate([cols2_high[modes:], cols2_low[modes:]], axis=1), twice(cross_wide)
        ) + dot(cols_add[modes:].astype(BF16), rest2_cross.astype(BF16))
        if not last:
            total = total + (gram_piece(6, ahead) + gram_piece(7, ahead))
        c_rr = pred_rr - taken
        c_vv = cols3[:modes]
        c_rv = cols3[modes:]
        c_vr = cols2[modes:].T + lax.dot_general(
            rest4, cols2_high[modes:], (((0,), (1,)), ((), ())), preferred_element_type=F32
        )

        pull = grads[pl.ds(here, 1), :] - jnp.sum(lam * pred_mean[0], axis=0, keepdims=True)
        mean_v = pred_mean[0] + jnp.sum(c_vv * pull, axis=1, keepdims=True)
        mean_r = pred_mean[1] + jnp.sum(c_rv * pull, axis=1, keepdims=True)
        means[pl.ds(here, 1), :] = diagonal(mean_v)
        diagonals[pl.ds(here, 1), :] = jnp.concatenate([diagonal(c_vv), diagonal(c_rr)], axis=1)
        rest4_f32 = rest4.astype(F32)
        bounds[pl.ds(jnp.minimum(step, 1), 1), :] = jnp.maximum(
            bounds[pl.ds(jnp.minimum(step, 1), 1), :], jnp.sum(rest4_f32 * rest4_f32, axis=0, keepdims=True)
        )

        if last:
            return carry
        a, b, c, d = columns[0], columns[1], columns[2], columns[3]
        pred_mean[0] = a * mean_v + b * mean_r
        pred_mean[1] = c * mean_v + d * mean_r
        g_vv = a * c_vv + b * c_rv
        g_vr = a * c_vr + b * c_rr
        g_rv = c * c_vv + d * c_rv
        g_rr = c * c_vr + d * c_rr
        p_vv[...] = g_vv * coef(0) + g_vr * coef(1) + eye * coef(4)
        p_rv[...] = g_rv * coef(0) + g_rr * coef(1) + eye * coef(5)
        p_vr[...] = g_vv * coef(2) + g_vr * coef(3) + eye * coef(5)
        p_rr[...] = g_rv * coef(2) + g_rr * coef(3) + eye * coef(6)
        gram_finish(total)
        return carry

    lax.fori_loop(0, steps - 1, one_step, 0)
    one_step(steps - 1, 0, last=True)

    def careful_step(step, carry):
        here = slot(step)
        total = gram_piece(0, here)
        for piece in range(1, PIECES):
            total = total + gram_piece(piece, here)
        gram_finish(total)
        low = scaled_t_ref[modes:, :] * mask_rows[pl.ds(here, 1), :].astype(BF16)
        lam_now[...] = lam_now[...] + dot(low, scaled_ref[:, modes:])
        floor = PIVOT_FLOOR * jnp.max(diagonal(lam_now[...]), axis=1, keepdims=True)
        rest_g[...] = grads[pl.ds(here, 1), :]

        def one_pivot(k, inner):
            lam = lam_now[...]
            lanes = lax.broadcasted_iota(jnp.int32, (1, modes), 1)
            pivots = diagonal(lam)
            pivot = jnp.max(pivots, axis=1, keepdims=True)
            place = jnp.min(jnp.where(pivots == pivot, lanes, modes), axis=1, keepdims=True)
            pick = jnp.where(lanes == place, 1.0, 0.0)
            used = pivot > floor
            inverse = jnp.where(used, 1.0 / jnp.where(used, pivot, 1.0), 0.0)
            lam_col = jnp.sum(lam * pick, axis=1, keepdims=True)
            lam_row = jnp.sum(lam * jnp.sum(eye * pick, axis=1, keepdims=True), axis=0, keepdims=True)
            seen_row = lam_row * inverse
            seen_col = lam_col * inverse
            c_row = jnp.sum(covar[:modes, :] * seen_col, axis=0, keepdims=True)
            c_col = jnp.sum(covar[:, :modes] * seen_row, axis=1, keepdims=True)
            spread = jnp.sum(c_row[:, :modes] * seen_row, axis=1, keepdims=True)
            gain = jnp.where(used, pivot, 0.0) / (1.0 + jnp.where(used, pivot, 0.0) * spread)
            reading = jnp.sum(rest_g[...] * pick, axis=1, keepdims=True) * inverse
            surprise = reading - jnp.sum(mean_row[:, :modes] * seen_row, axis=1, keepdims=True)
            mean_row[...] = mean_row[...] + c_row * (gain * surprise)
            covar[...] = covar[...] - c_col * (c_row * gain)
            rest_g[...] = rest_g[...] - lam_row * reading
            lam_now[...] = lam - lam_col * seen_row
            return inner

        lax.fori_loop(0, modes, one_pivot, 0)
        c_vv = covar[:modes, :modes]
        c_vr = covar[:modes, modes:]
        c_rv = covar[modes:, :modes]
        c_rr = covar[modes:, modes:]
        mean_v = mean_row[:, :modes]
        mean_r = mean_row[:, modes:]
        means[pl.ds(here, 1), :] = mean_v
        diagonals[pl.ds(here, 1), :] = jnp.concatenate([diagonal(c_vv), diagonal(c_rr)], axis=1)
        mean_row[...] = jnp.concatenate([coef(0) * mean_v + coef(1) * mean_r, coef(2) * mean_v + coef(3) * mean_r], axis=1)
        a, b, c, d = columns[0], columns[1], columns[2], columns[3]
        g_vv = a * c_vv + b * c_rv
        g_vr = a * c_vr + b * c_rr
        g_rv = c * c_vv + d * c_rv
        g_rr = c * c_vr + d * c_rr
        covar[:modes, :modes] = g_vv * coef(0) + g_vr * coef(1) + eye * coef(4)
        covar[:modes, modes:] = g_vv * coef(2) + g_vr * coef(3) + eye * coef(5)
        covar[modes:, :modes] = g_rv * coef(0) + g_rr * coef(1) + eye * coef(5)
        covar[modes:, modes:] = g_rv * coef(2) + g_rr * coef(3) + eye * coef(6)
        return carry

    limits = jnp.where(lax.broadcasted_iota(jnp.int32, bounds.shape, 0) == 0, LIMIT_FIRST**-2.0, LIMIT_LATER**-2.0)
    settled = jnp.max(jnp.sum(bounds[...] * limits, axis=1, keepdims=True)) <= 1.0

    @pl.when(jnp.logical_not(settled))
    def _():
        covar[...] = jnp.zeros(covar.shape, F32)
        covar[:modes, :modes] = eye * coef(7)
        covar[modes:, modes:] = eye * coef(7)
        mean_row[...] = jnp.zeros(mean_row.shape, F32)
        lax.fori_loop(0, steps, careful_step, 0)

    m_high, m_low = split(means[...])
    m_split = jnp.concatenate(
        [jnp.concatenate([m_high, m_high], axis=1), jnp.concatenate([m_low, m_low], axis=1)], axis=0
    )
    f_both = dot(m_split, scaled_t_ref[...])
    scaled_field = f_both[:steps] + f_both[steps:]
    field_ref[...] = scaled_field[:local] * (root_ref[...] * noise_ref[...])
    variances_ref[...] = diagonals[:local, :]
    gap = readings[...] - mask_rows[...] * scaled_field
    squares = gap * gap
    lanes_first = squares[:, :LANES]
    for chunk in range(1, chunks):
        lanes_first = lanes_first + squares[:, chunk * LANES : (chunk + 1) * LANES]
    row_sums[...] = lanes_first
    lane_total = row_sums[pl.ds(slot(0), 1), :]
    for step in range(1, steps):
        lane_total = lane_total + row_sums[pl.ds(slot(step), 1), :]
    misfit_ref[...] = jnp.sum(lane_total, axis=1, keepdims=True) / (steps * sensors)


def in_vmem(count):
    return [pl.BlockSpec(memory_space=pltpu.VMEM)] * count


def on_device(observations, block_mask, block_of_sensor, sensor_basis, noise_var, mode_rate, mode_var):
    local, sensors = observations.shape
    modes = sensor_basis.shape[1]
    blocks = block_mask.shape[1]
    count = lax.axis_size(AXIS)
    steps = count * local
    noise_row = noise_var.reshape(1, sensors)
    position = lax.axis_index(AXIS).astype(jnp.int32)

    prepare = pl.pallas_call(
        prepare_kernel,
        out_shape=(
            jax.ShapeDtypeStruct((2 * modes, sensors), BF16),
            jax.ShapeDtypeStruct((sensors, 2 * modes), BF16),
            jax.ShapeDtypeStruct((blocks, sensors), BF16),
            jax.ShapeDtypeStruct((8, modes), F32),
        ),
        in_specs=[pl.BlockSpec(memory_space=pl.ANY)] + in_vmem(3),
        out_specs=tuple(in_vmem(4)),
        scratch_shapes=[pltpu.VMEM((sensors, modes), F32), pltpu.SemaphoreType.DMA((COPIES,))],
        compiler_params=pltpu.CompilerParams(vmem_limit_bytes=44 * 2**20),
        cost_estimate=pl.CostEstimate(flops=2 * sensors * modes, bytes_accessed=12 * sensors * modes, transcendentals=sensors),
        name="prepare",
    )
    block_row = block_of_sensor.reshape(1, sensors)
    rate_row = mode_rate.reshape(1, modes)
    var_row = mode_var.reshape(1, modes)

    pieces, prepared = exchange(
        observations,
        block_mask,
        count,
        lambda noise: sensor_basis * lax.rsqrt(noise)[:, None],
        lambda scaled: prepare(scaled, block_row, rate_row, var_row),
        noise_var,
    )
    scaled_t, scaled, onehot, coefs = prepared

    square = pltpu.VMEM((modes, modes), F32)
    field, variances, misfit = pl.pallas_call(
        functools.partial(filter_kernel, count=count, local=local, blocks=blocks, parts=len(pieces)),
        out_shape=(
            jax.ShapeDtypeStruct((local, sensors), F32),
            jax.ShapeDtypeStruct((local, 2 * modes), F32),
            jax.ShapeDtypeStruct((1, 1), F32),
        ),
        in_specs=[pl.BlockSpec(memory_space=pltpu.SMEM)] + in_vmem(len(pieces) + 5),
        out_specs=tuple(in_vmem(3)),
        scratch_shapes=[
            square,
            square,
            square,
            square,
            pltpu.VMEM((2, modes, modes), F32),
            pltpu.VMEM((4, modes, modes), F32),
            square,
            pltpu.VMEM((1, sensors), F32),
            pltpu.VMEM((steps, sensors), F32),
            pltpu.VMEM((steps, sensors), F32),
            pltpu.VMEM((steps, modes), F32),
            pltpu.VMEM((steps, modes), F32),
            pltpu.VMEM((steps, 2 * modes), F32),
            pltpu.VMEM((8, modes), F32),
            pltpu.VMEM((steps, LANES), F32),
            pltpu.VMEM((2 * modes, 2 * modes), F32),
            pltpu.VMEM((1, 2 * modes), F32),
            pltpu.VMEM((1, modes), F32),
        ],
        compiler_params=pltpu.CompilerParams(vmem_limit_bytes=20 * 2**20),
        cost_estimate=pl.CostEstimate(flops=steps * sensors * modes * 512, bytes_accessed=8 * sensors * modes, transcendentals=0),
        name="filter",
    )(position.reshape(1), *pieces, onehot, scaled_t, scaled, noise_row, coefs)

    return (field, variances, misfit.reshape(1))


def solution(mesh):
    in_specs = (P(("groups", "tm"), None), P(("groups", "tm"), None), P(), P(), P(), P(), P())
    out_specs = (P(("groups", "tm"), None), P(("groups", "tm"), None), P("groups"))
    return jax.shard_map(on_device, mesh=mesh, in_specs=in_specs, out_specs=out_specs, check_vma=False)
```

```python
import functools

import jax
import jax.numpy as jnp
from jax import lax
from jax.experimental import pallas as pl
from jax.experimental.pallas import tpu as pltpu
from jax.sharding import PartitionSpec as P

BF16 = jnp.bfloat16
F32 = jnp.float32
AXIS = "tm"
LANES = 128
PIECES = 8
COPIES = 8
LIMIT_FIRST = 1.0e-2
LIMIT_LATER = 1.5e-3
PIVOT_FLOOR = 1.0e-6


def gather_rounds(count):
    bits = count.bit_length() - 1
    rounds = []
    top = bits
    if bits > 1 and (bits - 1) % 2 == 1:
        rounds.append((bits - 1, 1))
        top = bits - 1
    while top > 1:
        rounds.append((top - 2, 2))
        top -= 2
    if bits > 0:
        rounds.append((0, 1))
    return rounds


def swap(array, flip, count):
    return lax.ppermute(array, AXIS, [(p, p ^ flip) for p in range(count)])


def pack(observations, block_mask):
    local, sensors = observations.shape
    mask_row = jnp.pad(block_mask.astype(F32), ((0, 0), (0, LANES - block_mask.shape[1])))
    mask_tile = jnp.pad(mask_row.reshape(local, 1, LANES), ((0, 0), (0, 7), (0, 0)))
    return jnp.concatenate([observations.reshape(local, sensors // LANES, LANES), mask_tile], axis=1)


def exchange(observations, block_mask, count, early, late, seed):
    rounds = gather_rounds(count)
    pieces = [pack(observations, block_mask)]
    done = None
    for turn, (shift, width) in enumerate(rounds):
        flips = [digit << shift for digit in range(1, 1 << width)]
        rows = pieces[0] if turn == 0 else jnp.concatenate(pieces, axis=0)
        if turn == len(rounds) - 2:
            rows, seed = lax.optimization_barrier((rows, seed))
            seed = early(seed)
        if turn == len(rounds) - 1:
            rows, seed = lax.optimization_barrier((rows, seed))
            done = late(seed)
        if turn == 0:
            pieces = [rows] + [pack(swap(observations, flip, count), swap(block_mask, flip, count)) for flip in flips]
        else:
            pieces = [rows] + [swap(rows, flip, count) for flip in flips]
    return pieces, done


def slot_of(offset, count, local):
    slot = 0
    stride = local
    for shift, width in gather_rounds(count):
        slot = slot + ((offset >> shift) & ((1 << width) - 1)) * stride
        stride = stride << width
    return slot


def transition(mode_rate, mode_var):
    doubled = 2.0 * mode_rate
    damping = jnp.exp(-doubled)
    term_now = doubled * doubled * doubled / 6.0
    series = term_now
    for order in range(4, 15):
        term_now = term_now * doubled / order
        series = series + term_now
    q_value = mode_var * damping * series
    q_rate = mode_var * damping * (2.0 * doubled + series)
    q_cross = mode_var * damping * 2.0 * mode_rate * mode_rate
    root_value = jnp.sqrt(q_value)
    root_cross = q_cross / root_value
    root_rate = jnp.sqrt(q_value * q_rate - q_cross * q_cross) / root_value
    decay = jnp.exp(-mode_rate)
    return (
        decay * (1.0 + mode_rate),
        decay * mode_rate,
        -decay * mode_rate,
        decay * (1.0 - mode_rate),
        root_value,
        root_cross,
        root_rate,
        jnp.sqrt(mode_var),
    )


def split(x):
    high = x.astype(BF16)
    return high, (x - high.astype(F32)).astype(BF16)


def wide(x):
    return jnp.concatenate(split(x), axis=1)


def twice(x):
    return jnp.concatenate([x, x], axis=0)


def dot(left, right):
    return jnp.dot(left, right, preferred_element_type=F32)


def dot_split(left_wide, right_twice):
    both = dot(left_wide, right_twice)
    half = both.shape[1] // 2
    return both[:, :half] + both[:, half:]


def dot_three(left_wide, right):
    high, low = split(right)
    return dot(left_wide, twice(high)) + dot(left_wide[:, : high.shape[0]], low)


def prepare_kernel(
    basis_ref,
    block_ref,
    rate_ref,
    var_ref,
    scaled_t_ref,
    scaled_ref,
    onehot_ref,
    coef_ref,
    basis,
    arrivals,
):
    sensors, modes = basis_ref.shape
    depth = sensors // COPIES
    copies = []
    for part in range(COPIES):
        rows = pl.ds(part * depth, depth)
        copies.append(pltpu.make_async_copy(basis_ref.at[rows], basis.at[rows], arrivals.at[part]))
        copies[part].start()
    f_vv, f_vr, f_rv, f_rr, root_value, root_cross, root_rate, sigma_vec = transition(rate_ref[...], var_ref[...])
    rows = (
        f_vv,
        f_vr,
        f_rv,
        f_rr,
        root_value * root_value,
        root_value * root_cross,
        root_cross * root_cross + root_rate * root_rate,
        sigma_vec * sigma_vec,
    )
    coef_ref[...] = jnp.concatenate(rows, axis=0)
    block_index = lax.broadcasted_iota(jnp.int32, onehot_ref.shape, 0)
    onehot_ref[...] = jnp.where(block_index == block_ref[...], 1.0, 0.0).astype(BF16)
    for start in range(0, sensors, LANES):
        if start % depth == 0:
            copies[start // depth].wait()
        span = slice(start, start + LANES)
        chunk = basis[span, :]
        high, low = split(chunk.T)
        scaled_t_ref[:modes, span] = high
        scaled_t_ref[modes:, span] = low
        scaled_ref[span, :] = wide(chunk)


def filter_kernel(position_ref, *refs, count, local, blocks, parts):
    pieces = refs[:parts]
    (
        onehot_ref,
        scaled_t_ref,
        scaled_ref,
        noise_ref,
        coef_ref,
        field_ref,
        variances_ref,
        misfit_ref,
        p_vv,
        p_vr,
        p_rv,
        p_rr,
        pred_mean,
        columns,
        lam_now,
        lam_split,
        root_ref,
        mask_rows,
        readings,
        grads,
        means,
        diagonals,
        bounds,
        row_sums,
        covar,
        mean_row,
        rest_g,
    ) = refs[parts:]
    modes = scaled_t_ref.shape[0] // 2
    sensors = scaled_t_ref.shape[1]
    piece_rows = pieces[0].shape[0]
    steps = parts * piece_rows
    chunks = sensors // LANES
    position = position_ref[0]
    row_index = lax.broadcasted_iota(jnp.int32, (modes, modes), 0)
    col_index = lax.broadcasted_iota(jnp.int32, (modes, modes), 1)
    eye = jnp.where(row_index == col_index, 1.0, 0.0).astype(F32)

    def coef(k):
        return coef_ref[k : k + 1, :]

    def slot(step):
        return slot_of((step // local) ^ position, count, local) + step % local

    def diagonal(square):
        return jnp.sum(eye * square, axis=0, keepdims=True)

    root_ref[...] = lax.rsqrt(noise_ref[...])
    masks = jnp.concatenate([ref[:, chunks, :blocks] for ref in pieces], axis=0).astype(BF16)
    mask_rows[...] = dot(masks, onehot_ref[...])
    for chunk in range(chunks):
        span = slice(chunk * LANES, (chunk + 1) * LANES)
        rows = jnp.concatenate([ref[:, chunk, :] for ref in pieces], axis=0)
        readings[:, span] = mask_rows[:, span] * rows * root_ref[:, span]
    for k in range(4):
        columns[k] = jnp.broadcast_to(jnp.sum(eye * coef(k), axis=1, keepdims=True), (modes, modes))
    stationary = eye * coef(7)
    p_vv[...] = stationary
    p_rr[...] = stationary
    p_vr[...] = jnp.zeros((modes, modes), F32)
    p_rv[...] = jnp.zeros((modes, modes), F32)
    pred_mean[...] = jnp.zeros(pred_mean.shape, F32)
    bounds[...] = jnp.zeros(bounds.shape, F32)

    depth = sensors // PIECES

    def gram_piece(piece, at):
        span = slice(piece * depth, (piece + 1) * depth)
        left = scaled_t_ref[:modes, span] * mask_rows[pl.ds(at, 1), span].astype(BF16)
        return dot(left, scaled_ref[span, :])

    def gram_finish(total):
        cross = total[:, modes:]
        lam = total[:, :modes] + cross + cross.T
        lam_now[...] = lam
        lam_split[...] = wide(lam)

    first_left = scaled_t_ref[:modes, :] * mask_rows[pl.ds(slot(0), 1), :].astype(BF16)
    y_high, y_low = split(readings[...])
    first = dot(jnp.concatenate([first_left, y_high, y_low], axis=0), scaled_ref[...])
    gram_finish(first[:modes])
    g_half = first[modes:, :modes] + first[modes:, modes:]
    grads[...] = g_half[:steps] + g_half[steps:]

    def one_step(step, carry, last=False):
        here = slot(step)
        ahead = slot(step + 1)
        lam = lam_now[...]
        pred_vv = p_vv[...]
        pred_rv = p_rv[...]
        pred_rr = p_rr[...]
        lam_wide = lam_split[...]
        lam_p = dot_three(lam_wide, pred_vv)
        cross = dot_three(lam_wide, p_vr[...])
        total = None if last else gram_piece(0, ahead) + gram_piece(1, ahead)
        scale = 1.0 / (1.0 + diagonal(lam) * diagonal(pred_vv))
        rest = eye * (1.0 - scale) - lam_p * scale
        scaled_p = jnp.concatenate([pred_vv * scale, pred_rv * scale], axis=0)
        second = dot_split(wide(jnp.concatenate([rest, scaled_p], axis=0)), twice(wide(rest)))
        if not last:
            total = total + (gram_piece(2, ahead) + gram_piece(3, ahead))
        rest2 = second[:modes]
        cols1 = scaled_p + second[modes:]
        rest2_high = rest2.astype(BF16)
        cross_high, cross_low = split(cross)
        rest4 = dot(rest2_high, rest2_high).astype(BF16)
        rest2_cross = dot(rest2_high, cross_high)
        cols_add = dot(cols1.astype(BF16), rest2_high)
        if not last:
            total = total + (gram_piece(4, ahead) + gram_piece(5, ahead))
        cols2 = cols1 + cols_add
        cols2_high, cols2_low = split(cols2)
        cols3 = cols2 + dot(cols2_high, rest4)
        cross_wide = jnp.concatenate([cross_high, cross_low], axis=1)
        taken = dot_split(
            jnp.concatenate([cols2_high[modes:], cols2_low[modes:]], axis=1), twice(cross_wide)
        ) + dot(cols_add[modes:].astype(BF16), rest2_cross.astype(BF16))
        if not last:
            total = total + (gram_piece(6, ahead) + gram_piece(7, ahead))
        c_rr = pred_rr - taken
        c_vv = cols3[:modes]
        c_rv = cols3[modes:]
        c_vr = cols2[modes:].T + lax.dot_general(
            rest4, cols2_high[modes:], (((0,), (1,)), ((), ())), preferred_element_type=F32
        )

        pull = grads[pl.ds(here, 1), :] - jnp.sum(lam * pred_mean[0], axis=0, keepdims=True)
        mean_v = pred_mean[0] + jnp.sum(c_vv * pull, axis=1, keepdims=True)
        mean_r = pred_mean[1] + jnp.sum(c_rv * pull, axis=1, keepdims=True)
        means[pl.ds(here, 1), :] = diagonal(mean_v)
        diagonals[pl.ds(here, 1), :] = jnp.concatenate([diagonal(c_vv), diagonal(c_rr)], axis=1)
        rest4_f32 = rest4.astype(F32)
        bounds[pl.ds(jnp.minimum(step, 1), 1), :] = jnp.maximum(
            bounds[pl.ds(jnp.minimum(step, 1), 1), :], jnp.sum(rest4_f32 * rest4_f32, axis=0, keepdims=True)
        )

        if last:
            return carry
        a, b, c, d = columns[0], columns[1], columns[2], columns[3]
        pred_mean[0] = a * mean_v + b * mean_r
        pred_mean[1] = c * mean_v + d * mean_r
        g_vv = a * c_vv + b * c_rv
        g_vr = a * c_vr + b * c_rr
        g_rv = c * c_vv + d * c_rv
        g_rr = c * c_vr + d * c_rr
        p_vv[...] = g_vv * coef(0) + g_vr * coef(1) + eye * coef(4)
        p_rv[...] = g_rv * coef(0) + g_rr * coef(1) + eye * coef(5)
        p_vr[...] = g_vv * coef(2) + g_vr * coef(3) + eye * coef(5)
        p_rr[...] = g_rv * coef(2) + g_rr * coef(3) + eye * coef(6)
        gram_finish(total)
        return carry

    lax.fori_loop(0, steps - 1, one_step, 0)
    one_step(steps - 1, 0, last=True)

    def careful_step(step, carry):
        here = slot(step)
        total = gram_piece(0, here)
        for piece in range(1, PIECES):
            total = total + gram_piece(piece, here)
        gram_finish(total)
        low = scaled_t_ref[modes:, :] * mask_rows[pl.ds(here, 1), :].astype(BF16)
        lam_now[...] = lam_now[...] + dot(low, scaled_ref[:, modes:])
        floor = PIVOT_FLOOR * jnp.max(diagonal(lam_now[...]), axis=1, keepdims=True)
        rest_g[...] = grads[pl.ds(here, 1), :]

        def one_pivot(k, inner):
            lam = lam_now[...]
            lanes = lax.broadcasted_iota(jnp.int32, (1, modes), 1)
            pivots = diagonal(lam)
            pivot = jnp.max(pivots, axis=1, keepdims=True)
            place = jnp.min(jnp.where(pivots == pivot, lanes, modes), axis=1, keepdims=True)
            pick = jnp.where(lanes == place, 1.0, 0.0)
            used = pivot > floor
            inverse = jnp.where(used, 1.0 / jnp.where(used, pivot, 1.0), 0.0)
            lam_col = jnp.sum(lam * pick, axis=1, keepdims=True)
            lam_row = jnp.sum(lam * jnp.sum(eye * pick, axis=1, keepdims=True), axis=0, keepdims=True)
            seen_row = lam_row * inverse
            seen_col = lam_col * inverse
            c_row = jnp.sum(covar[:modes, :] * seen_col, axis=0, keepdims=True)
            c_col = jnp.sum(covar[:, :modes] * seen_row, axis=1, keepdims=True)
            spread = jnp.sum(c_row[:, :modes] * seen_row, axis=1, keepdims=True)
            gain = jnp.where(used, pivot, 0.0) / (1.0 + jnp.where(used, pivot, 0.0) * spread)
            reading = jnp.sum(rest_g[...] * pick, axis=1, keepdims=True) * inverse
            surprise = reading - jnp.sum(mean_row[:, :modes] * seen_row, axis=1, keepdims=True)
            mean_row[...] = mean_row[...] + c_row * (gain * surprise)
            covar[...] = covar[...] - c_col * (c_row * gain)
            rest_g[...] = rest_g[...] - lam_row * reading
            lam_now[...] = lam - lam_col * seen_row
            return inner

        lax.fori_loop(0, modes, one_pivot, 0)
        c_vv = covar[:modes, :modes]
        c_vr = covar[:modes, modes:]
        c_rv = covar[modes:, :modes]
        c_rr = covar[modes:, modes:]
        mean_v = mean_row[:, :modes]
        mean_r = mean_row[:, modes:]
        means[pl.ds(here, 1), :] = mean_v
        diagonals[pl.ds(here, 1), :] = jnp.concatenate([diagonal(c_vv), diagonal(c_rr)], axis=1)
        mean_row[...] = jnp.concatenate([coef(0) * mean_v + coef(1) * mean_r, coef(2) * mean_v + coef(3) * mean_r], axis=1)
        a, b, c, d = columns[0], columns[1], columns[2], columns[3]
        g_vv = a * c_vv + b * c_rv
        g_vr = a * c_vr + b * c_rr
        g_rv = c * c_vv + d * c_rv
        g_rr = c * c_vr + d * c_rr
        covar[:modes, :modes] = g_vv * coef(0) + g_vr * coef(1) + eye * coef(4)
        covar[:modes, modes:] = g_vv * coef(2) + g_vr * coef(3) + eye * coef(5)
        covar[modes:, :modes] = g_rv * coef(0) + g_rr * coef(1) + eye * coef(5)
        covar[modes:, modes:] = g_rv * coef(2) + g_rr * coef(3) + eye * coef(6)
        return carry

    limits = jnp.where(lax.broadcasted_iota(jnp.int32, bounds.shape, 0) == 0, LIMIT_FIRST**-2.0, LIMIT_LATER**-2.0)
    settled = jnp.max(jnp.sum(bounds[...] * limits, axis=1, keepdims=True)) <= 1.0

    @pl.when(jnp.logical_not(settled))
    def _():
        covar[...] = jnp.zeros(covar.shape, F32)
        covar[:modes, :modes] = eye * coef(7)
        covar[modes:, modes:] = eye * coef(7)
        mean_row[...] = jnp.zeros(mean_row.shape, F32)
        lax.fori_loop(0, steps, careful_step, 0)

    m_high, m_low = split(means[...])
    m_split = jnp.concatenate(
        [jnp.concatenate([m_high, m_high], axis=1), jnp.concatenate([m_low, m_low], axis=1)], axis=0
    )
    f_both = dot(m_split, scaled_t_ref[...])
    scaled_field = f_both[:steps] + f_both[steps:]
    field_ref[...] = scaled_field[:local] * (root_ref[...] * noise_ref[...])
    variances_ref[...] = diagonals[:local, :]
    gap = readings[...] - mask_rows[...] * scaled_field
    squares = gap * gap
    lanes_first = squares[:, :LANES]
    for chunk in range(1, chunks):
        lanes_first = lanes_first + squares[:, chunk * LANES : (chunk + 1) * LANES]
    row_sums[...] = lanes_first
    lane_total = row_sums[pl.ds(slot(0), 1), :]
    for step in range(1, steps):
        lane_total = lane_total + row_sums[pl.ds(slot(step), 1), :]
    misfit_ref[...] = jnp.sum(lane_total, axis=1, keepdims=True) / (steps * sensors)


def in_vmem(count):
    return [pl.BlockSpec(memory_space=pltpu.VMEM)] * count


def on_device(observations, block_mask, block_of_sensor, sensor_basis, noise_var, mode_rate, mode_var):
    local, sensors = observations.shape
    modes = sensor_basis.shape[1]
    blocks = block_mask.shape[1]
    count = lax.axis_size(AXIS)
    steps = count * local
    noise_row = noise_var.reshape(1, sensors)
    position = lax.axis_index(AXIS).astype(jnp.int32)

    prepare = pl.pallas_call(
        prepare_kernel,
        out_shape=(
            jax.ShapeDtypeStruct((2 * modes, sensors), BF16),
            jax.ShapeDtypeStruct((sensors, 2 * modes), BF16),
            jax.ShapeDtypeStruct((blocks, sensors), BF16),
            jax.ShapeDtypeStruct((8, modes), F32),
        ),
        in_specs=[pl.BlockSpec(memory_space=pl.ANY)] + in_vmem(3),
        out_specs=tuple(in_vmem(4)),
        scratch_shapes=[pltpu.VMEM((sensors, modes), F32), pltpu.SemaphoreType.DMA((COPIES,))],
        compiler_params=pltpu.CompilerParams(vmem_limit_bytes=44 * 2**20),
        cost_estimate=pl.CostEstimate(flops=2 * sensors * modes, bytes_accessed=12 * sensors * modes, transcendentals=sensors),
        name="prepare",
    )
    block_row = block_of_sensor.reshape(1, sensors)
    rate_row = mode_rate.reshape(1, modes)
    var_row = mode_var.reshape(1, modes)

    pieces, prepared = exchange(
        observations,
        block_mask,
        count,
        lambda noise: sensor_basis * lax.rsqrt(noise)[:, None],
        lambda scaled: prepare(scaled, block_row, rate_row, var_row),
        noise_var,
    )
    scaled_t, scaled, onehot, coefs = prepared

    square = pltpu.VMEM((modes, modes), F32)
    field, variances, misfit = pl.pallas_call(
        functools.partial(filter_kernel, count=count, local=local, blocks=blocks, parts=len(pieces)),
        out_shape=(
            jax.ShapeDtypeStruct((local, sensors), F32),
            jax.ShapeDtypeStruct((local, 2 * modes), F32),
            jax.ShapeDtypeStruct((1, 1), F32),
        ),
        in_specs=[pl.BlockSpec(memory_space=pltpu.SMEM)] + in_vmem(len(pieces) + 5),
        out_specs=tuple(in_vmem(3)),
        scratch_shapes=[
            square,
            square,
            square,
            square,
            pltpu.VMEM((2, modes, modes), F32),
            pltpu.VMEM((4, modes, modes), F32),
            square,
            pltpu.VMEM((modes, 2 * modes), BF16),
            pltpu.VMEM((1, sensors), F32),
            pltpu.VMEM((steps, sensors), F32),
            pltpu.VMEM((steps, sensors), F32),
            pltpu.VMEM((steps, modes), F32),
            pltpu.VMEM((steps, modes), F32),
            pltpu.VMEM((steps, 2 * modes), F32),
            pltpu.VMEM((8, modes), F32),
            pltpu.VMEM((steps, LANES), F32),
            pltpu.VMEM((2 * modes, 2 * modes), F32),
            pltpu.VMEM((1, 2 * modes), F32),
            pltpu.VMEM((1, modes), F32),
        ],
        compiler_params=pltpu.CompilerParams(vmem_limit_bytes=20 * 2**20),
        cost_estimate=pl.CostEstimate(flops=steps * sensors * modes * 512, bytes_accessed=8 * sensors * modes, transcendentals=0),
        name="filter",
    )(position.reshape(1), *pieces, onehot, scaled_t, scaled, noise_row, coefs)

    return (field, variances, misfit.reshape(1))


def solution(mesh):
    in_specs = (P(("groups", "tm"), None), P(("groups", "tm"), None), P(), P(), P(), P(), P())
    out_specs = (P(("groups", "tm"), None), P(("groups", "tm"), None), P("groups"))
    return jax.shard_map(on_device, mesh=mesh, in_specs=in_specs, out_specs=out_specs, check_vma=False)
```

```python
import functools

import jax
import jax.numpy as jnp
from jax import lax
from jax.experimental import pallas as pl
from jax.experimental.pallas import tpu as pltpu
from jax.sharding import PartitionSpec as P

BF16 = jnp.bfloat16
F32 = jnp.float32
AXIS = "tm"
LANES = 128
PIECES = 8
COPIES = 8
LIMIT_FIRST = 1.0e-2
LIMIT_LATER = 1.5e-3
PIVOT_FLOOR = 1.0e-6


def gather_rounds(count):
    bits = count.bit_length() - 1
    rounds = []
    top = bits
    if bits > 1 and (bits - 1) % 2 == 1:
        rounds.append((bits - 1, 1))
        top = bits - 1
    while top > 1:
        rounds.append((top - 2, 2))
        top -= 2
    if bits > 0:
        rounds.append((0, 1))
    return rounds


def swap(array, flip, count):
    return lax.ppermute(array, AXIS, [(p, p ^ flip) for p in range(count)])


def pack(observations, block_mask):
    local, sensors = observations.shape
    mask_row = jnp.pad(block_mask.astype(F32), ((0, 0), (0, LANES - block_mask.shape[1])))
    mask_tile = jnp.pad(mask_row.reshape(local, 1, LANES), ((0, 0), (0, 7), (0, 0)))
    return jnp.concatenate([observations.reshape(local, sensors // LANES, LANES), mask_tile], axis=1)


def exchange(observations, block_mask, count, early, late, seed):
    rounds = gather_rounds(count)
    pieces = [pack(observations, block_mask)]
    done = None
    for turn, (shift, width) in enumerate(rounds):
        flips = [digit << shift for digit in range(1, 1 << width)]
        rows = pieces[0] if turn == 0 else jnp.concatenate(pieces, axis=0)
        if turn == len(rounds) - 2:
            rows, seed = lax.optimization_barrier((rows, seed))
            seed = early(seed)
        if turn == len(rounds) - 1:
            rows, seed = lax.optimization_barrier((rows, seed))
            done = late(seed)
        if turn == 0:
            pieces = [rows] + [pack(swap(observations, flip, count), swap(block_mask, flip, count)) for flip in flips]
        else:
            pieces = [rows] + [swap(rows, flip, count) for flip in flips]
    return pieces, done


def slot_of(offset, count, local):
    slot = 0
    stride = local
    for shift, width in gather_rounds(count):
        slot = slot + ((offset >> shift) & ((1 << width) - 1)) * stride
        stride = stride << width
    return slot


def transition(mode_rate, mode_var):
    doubled = 2.0 * mode_rate
    damping = jnp.exp(-doubled)
    term_now = doubled * doubled * doubled / 6.0
    series = term_now
    for order in range(4, 15):
        term_now = term_now * doubled / order
        series = series + term_now
    q_value = mode_var * damping * series
    q_rate = mode_var * damping * (2.0 * doubled + series)
    q_cross = mode_var * damping * 2.0 * mode_rate * mode_rate
    root_value = jnp.sqrt(q_value)
    root_cross = q_cross / root_value
    root_rate = jnp.sqrt(q_value * q_rate - q_cross * q_cross) / root_value
    decay = jnp.exp(-mode_rate)
    return (
        decay * (1.0 + mode_rate),
        decay * mode_rate,
        -decay * mode_rate,
        decay * (1.0 - mode_rate),
        root_value,
        root_cross,
        root_rate,
        jnp.sqrt(mode_var),
    )


def split(x):
    high = x.astype(BF16)
    return high, (x - high.astype(F32)).astype(BF16)


def wide(x):
    return jnp.concatenate(split(x), axis=1)


def twice(x):
    return jnp.concatenate([x, x], axis=0)


def dot(left, right):
    return jnp.dot(left, right, preferred_element_type=F32)


def dot_split(left_wide, right_twice):
    both = dot(left_wide, right_twice)
    half = both.shape[1] // 2
    return both[:, :half] + both[:, half:]


def dot_three(left_wide, right):
    high, low = split(right)
    return dot(left_wide, twice(high)) + dot(left_wide[:, : high.shape[0]], low)


def prepare_kernel(
    basis_ref,
    block_ref,
    rate_ref,
    var_ref,
    scaled_t_ref,
    scaled_ref,
    onehot_ref,
    coef_ref,
    basis,
    arrivals,
):
    sensors, modes = basis_ref.shape
    depth = sensors // COPIES
    copies = []
    for part in range(COPIES):
        rows = pl.ds(part * depth, depth)
        copies.append(pltpu.make_async_copy(basis_ref.at[rows], basis.at[rows], arrivals.at[part]))
        copies[part].start()
    f_vv, f_vr, f_rv, f_rr, root_value, root_cross, root_rate, sigma_vec = transition(rate_ref[...], var_ref[...])
    rows = (
        f_vv,
        f_vr,
        f_rv,
        f_rr,
        root_value * root_value,
        root_value * root_cross,
        root_cross * root_cross + root_rate * root_rate,
        sigma_vec * sigma_vec,
    )
    coef_ref[...] = jnp.concatenate(rows, axis=0)
    block_index = lax.broadcasted_iota(jnp.int32, onehot_ref.shape, 0)
    onehot_ref[...] = jnp.where(block_index == block_ref[...], 1.0, 0.0).astype(BF16)
    for start in range(0, sensors, LANES):
        if start % depth == 0:
            copies[start // depth].wait()
        span = slice(start, start + LANES)
        chunk = basis[span, :]
        high, low = split(chunk.T)
        scaled_t_ref[:modes, span] = high
        scaled_t_ref[modes:, span] = low
        scaled_ref[span, :] = wide(chunk)


def filter_kernel(position_ref, *refs, count, local, blocks, parts):
    pieces = refs[:parts]
    (
        onehot_ref,
        scaled_t_ref,
        scaled_ref,
        noise_ref,
        coef_ref,
        field_ref,
        variances_ref,
        misfit_ref,
        p_vv,
        p_vr,
        p_rv,
        p_rr,
        pred_mean,
        columns,
        lam_now,
        root_ref,
        mask_rows,
        readings,
        grads,
        means,
        diagonals,
        bounds,
        row_sums,
        covar,
        mean_row,
        rest_g,
    ) = refs[parts:]
    modes = scaled_t_ref.shape[0] // 2
    sensors = scaled_t_ref.shape[1]
    piece_rows = pieces[0].shape[0]
    steps = parts * piece_rows
    chunks = sensors // LANES
    position = position_ref[0]
    row_index = lax.broadcasted_iota(jnp.int32, (modes, modes), 0)
    col_index = lax.broadcasted_iota(jnp.int32, (modes, modes), 1)
    eye = jnp.where(row_index == col_index, 1.0, 0.0).astype(F32)

    def coef(k):
        return coef_ref[k : k + 1, :]

    def slot(step):
        return slot_of((step // local) ^ position, count, local) + step % local

    def diagonal(square):
        return jnp.sum(eye * square, axis=0, keepdims=True)

    root_ref[...] = lax.rsqrt(noise_ref[...])
    masks = jnp.concatenate([ref[:, chunks, :blocks] for ref in pieces], axis=0).astype(BF16)
    mask_rows[...] = dot(masks, onehot_ref[...])
    for chunk in range(chunks):
        span = slice(chunk * LANES, (chunk + 1) * LANES)
        rows = jnp.concatenate([ref[:, chunk, :] for ref in pieces], axis=0)
        readings[:, span] = mask_rows[:, span] * rows * root_ref[:, span]
    for k in range(4):
        columns[k] = jnp.broadcast_to(jnp.sum(eye * coef(k), axis=1, keepdims=True), (modes, modes))
    stationary = eye * coef(7)
    p_vv[...] = stationary
    p_rr[...] = stationary
    p_vr[...] = jnp.zeros((modes, modes), F32)
    p_rv[...] = jnp.zeros((modes, modes), F32)
    pred_mean[...] = jnp.zeros(pred_mean.shape, F32)
    bounds[...] = jnp.zeros(bounds.shape, F32)

    depth = sensors // PIECES

    def gram_piece(piece, at):
        span = slice(piece * depth, (piece + 1) * depth)
        left = scaled_t_ref[:modes, span] * mask_rows[pl.ds(at, 1), span].astype(BF16)
        return dot(left, scaled_ref[span, :])

    def gram_finish(total):
        cross = total[:, modes:]
        lam_now[...] = total[:, :modes] + cross + cross.T

    first_left = scaled_t_ref[:modes, :] * mask_rows[pl.ds(slot(0), 1), :].astype(BF16)
    y_high, y_low = split(readings[...])
    first = dot(jnp.concatenate([first_left, y_high, y_low], axis=0), scaled_ref[...])
    gram_finish(first[:modes])
    g_half = first[modes:, :modes] + first[modes:, modes:]
    grads[...] = g_half[:steps] + g_half[steps:]

    def one_step(step, carry, last=False):
        here = slot(step)
        ahead = slot(step + 1)
        lam = lam_now[...]
        pred_vv = p_vv[...]
        pred_rv = p_rv[...]
        pred_rr = p_rr[...]
        lam_wide = wide(lam)
        lam_p = dot_three(lam_wide, pred_vv)
        cross = dot_three(lam_wide, p_vr[...])
        total = None if last else gram_piece(0, ahead) + gram_piece(1, ahead)
        scale = 1.0 / (1.0 + diagonal(lam) * diagonal(pred_vv))
        rest = eye * (1.0 - scale) - lam_p * scale
        scaled_p = jnp.concatenate([pred_vv * scale, pred_rv * scale], axis=0)
        second = dot_split(wide(jnp.concatenate([rest, scaled_p], axis=0)), twice(wide(rest)))
        if not last:
            total = total + (gram_piece(2, ahead) + gram_piece(3, ahead))
        rest2 = second[:modes]
        cols1 = scaled_p + second[modes:]
        rest2_high = rest2.astype(BF16)
        cross_high, cross_low = split(cross)
        rest4 = dot(rest2_high, rest2_high).astype(BF16)
        rest2_cross = dot(rest2_high, cross_high)
        cols_add = dot(cols1.astype(BF16), rest2_high)
        if not last:
            total = total + (gram_piece(4, ahead) + gram_piece(5, ahead))
        cols2 = cols1 + cols_add
        cols2_high, cols2_low = split(cols2)
        cols3 = cols2 + dot(cols2_high, rest4)
        cross_wide = jnp.concatenate([cross_high, cross_low], axis=1)
        taken = dot_split(
            jnp.concatenate([cols2_high[modes:], cols2_low[modes:]], axis=1), twice(cross_wide)
        ) + dot(cols_add[modes:].astype(BF16), rest2_cross.astype(BF16))
        if not last:
            total = total + (gram_piece(6, ahead) + gram_piece(7, ahead))
        c_rr = pred_rr - taken
        c_vv = cols3[:modes]
        c_rv = cols3[modes:]
        c_vr = cols2[modes:].T + lax.dot_general(
            rest4, cols2_high[modes:], (((0,), (1,)), ((), ())), preferred_element_type=F32
        )

        pull = grads[pl.ds(here, 1), :] - jnp.sum(lam * pred_mean[0], axis=0, keepdims=True)
        mean_v = pred_mean[0] + jnp.sum(c_vv * pull, axis=1, keepdims=True)
        mean_r = pred_mean[1] + jnp.sum(c_rv * pull, axis=1, keepdims=True)
        means[pl.ds(here, 1), :] = diagonal(mean_v)
        diagonals[pl.ds(here, 1), :] = jnp.concatenate([diagonal(c_vv), diagonal(c_rr)], axis=1)
        rest4_f32 = rest4.astype(F32)
        bounds[pl.ds(jnp.minimum(step, 1), 1), :] = jnp.maximum(
            bounds[pl.ds(jnp.minimum(step, 1), 1), :], jnp.sum(rest4_f32 * rest4_f32, axis=0, keepdims=True)
        )

        if last:
            return carry
        a, b, c, d = columns[0], columns[1], columns[2], columns[3]
        pred_mean[0] = a * mean_v + b * mean_r
        pred_mean[1] = c * mean_v + d * mean_r
        g_vv = a * c_vv + b * c_rv
        g_vr = a * c_vr + b * c_rr
        g_rv = c * c_vv + d * c_rv
        g_rr = c * c_vr + d * c_rr
        p_vv[...] = g_vv * coef(0) + g_vr * coef(1) + eye * coef(4)
        p_rv[...] = g_rv * coef(0) + g_rr * coef(1) + eye * coef(5)
        p_vr[...] = g_vv * coef(2) + g_vr * coef(3) + eye * coef(5)
        p_rr[...] = g_rv * coef(2) + g_rr * coef(3) + eye * coef(6)
        gram_finish(total)
        return carry

    lax.fori_loop(0, steps - 1, one_step, 0)
    one_step(steps - 1, 0, last=True)

    def careful_step(step, carry):
        here = slot(step)
        total = gram_piece(0, here)
        for piece in range(1, PIECES):
            total = total + gram_piece(piece, here)
        gram_finish(total)
        low = scaled_t_ref[modes:, :] * mask_rows[pl.ds(here, 1), :].astype(BF16)
        lam_now[...] = lam_now[...] + dot(low, scaled_ref[:, modes:])
        floor = PIVOT_FLOOR * jnp.max(diagonal(lam_now[...]), axis=1, keepdims=True)
        rest_g[...] = grads[pl.ds(here, 1), :]

        def one_pivot(k, inner):
            lam = lam_now[...]
            lanes = lax.broadcasted_iota(jnp.int32, (1, modes), 1)
            pivots = diagonal(lam)
            pivot = jnp.max(pivots, axis=1, keepdims=True)
            place = jnp.min(jnp.where(pivots == pivot, lanes, modes), axis=1, keepdims=True)
            pick = jnp.where(lanes == place, 1.0, 0.0)
            used = pivot > floor
            inverse = jnp.where(used, 1.0 / jnp.where(used, pivot, 1.0), 0.0)
            lam_col = jnp.sum(lam * pick, axis=1, keepdims=True)
            lam_row = jnp.sum(lam * jnp.sum(eye * pick, axis=1, keepdims=True), axis=0, keepdims=True)
            seen_row = lam_row * inverse
            seen_col = lam_col * inverse
            c_row = jnp.sum(covar[:modes, :] * seen_col, axis=0, keepdims=True)
            c_col = jnp.sum(covar[:, :modes] * seen_row, axis=1, keepdims=True)
            spread = jnp.sum(c_row[:, :modes] * seen_row, axis=1, keepdims=True)
            gain = jnp.where(used, pivot, 0.0) / (1.0 + jnp.where(used, pivot, 0.0) * spread)
            reading = jnp.sum(rest_g[...] * pick, axis=1, keepdims=True) * inverse
            surprise = reading - jnp.sum(mean_row[:, :modes] * seen_row, axis=1, keepdims=True)
            mean_row[...] = mean_row[...] + c_row * (gain * surprise)
            covar[...] = covar[...] - c_col * (c_row * gain)
            rest_g[...] = rest_g[...] - lam_row * reading
            lam_now[...] = lam - lam_col * seen_row
            return inner

        lax.fori_loop(0, modes, one_pivot, 0)
        c_vv = covar[:modes, :modes]
        c_vr = covar[:modes, modes:]
        c_rv = covar[modes:, :modes]
        c_rr = covar[modes:, modes:]
        mean_v = mean_row[:, :modes]
        mean_r = mean_row[:, modes:]
        means[pl.ds(here, 1), :] = mean_v
        diagonals[pl.ds(here, 1), :] = jnp.concatenate([diagonal(c_vv), diagonal(c_rr)], axis=1)
        mean_row[...] = jnp.concatenate([coef(0) * mean_v + coef(1) * mean_r, coef(2) * mean_v + coef(3) * mean_r], axis=1)
        a, b, c, d = columns[0], columns[1], columns[2], columns[3]
        g_vv = a * c_vv + b * c_rv
        g_vr = a * c_vr + b * c_rr
        g_rv = c * c_vv + d * c_rv
        g_rr = c * c_vr + d * c_rr
        covar[:modes, :modes] = g_vv * coef(0) + g_vr * coef(1) + eye * coef(4)
        covar[:modes, modes:] = g_vv * coef(2) + g_vr * coef(3) + eye * coef(5)
        covar[modes:, :modes] = g_rv * coef(0) + g_rr * coef(1) + eye * coef(5)
        covar[modes:, modes:] = g_rv * coef(2) + g_rr * coef(3) + eye * coef(6)
        return carry

    limits = jnp.where(lax.broadcasted_iota(jnp.int32, bounds.shape, 0) == 0, LIMIT_FIRST**-2.0, LIMIT_LATER**-2.0)
    settled = jnp.max(jnp.sum(bounds[...] * limits, axis=1, keepdims=True)) <= 1.0

    @pl.when(jnp.logical_not(settled))
    def _():
        covar[...] = jnp.zeros(covar.shape, F32)
        covar[:modes, :modes] = eye * coef(7)
        covar[modes:, modes:] = eye * coef(7)
        mean_row[...] = jnp.zeros(mean_row.shape, F32)
        lax.fori_loop(0, steps, careful_step, 0)

    m_high, m_low = split(means[...])
    m_split = jnp.concatenate(
        [jnp.concatenate([m_high, m_high], axis=1), jnp.concatenate([m_low, m_low], axis=1)], axis=0
    )
    f_both = dot(m_split, scaled_t_ref[...])
    scaled_field = f_both[:steps] + f_both[steps:]
    field_ref[...] = scaled_field[:local] * (root_ref[...] * noise_ref[...])
    variances_ref[...] = diagonals[:local, :]
    lanes_first = jnp.zeros((steps, LANES), F32)
    for chunk in range(chunks):
        span = slice(chunk * LANES, (chunk + 1) * LANES)
        gap = readings[:, span] - mask_rows[:, span] * scaled_field[:, span]
        lanes_first = lanes_first + gap * gap
    row_sums[...] = lanes_first
    lane_total = row_sums[pl.ds(slot(0), 1), :]
    for step in range(1, steps):
        lane_total = lane_total + row_sums[pl.ds(slot(step), 1), :]
    misfit_ref[...] = jnp.sum(lane_total, axis=1, keepdims=True) / (steps * sensors)


def in_vmem(count):
    return [pl.BlockSpec(memory_space=pltpu.VMEM)] * count


def on_device(observations, block_mask, block_of_sensor, sensor_basis, noise_var, mode_rate, mode_var):
    local, sensors = observations.shape
    modes = sensor_basis.shape[1]
    blocks = block_mask.shape[1]
    count = lax.axis_size(AXIS)
    steps = count * local
    noise_row = noise_var.reshape(1, sensors)
    position = lax.axis_index(AXIS).astype(jnp.int32)

    prepare = pl.pallas_call(
        prepare_kernel,
        out_shape=(
            jax.ShapeDtypeStruct((2 * modes, sensors), BF16),
            jax.ShapeDtypeStruct((sensors, 2 * modes), BF16),
            jax.ShapeDtypeStruct((blocks, sensors), BF16),
            jax.ShapeDtypeStruct((8, modes), F32),
        ),
        in_specs=[pl.BlockSpec(memory_space=pl.ANY)] + in_vmem(3),
        out_specs=tuple(in_vmem(4)),
        scratch_shapes=[pltpu.VMEM((sensors, modes), F32), pltpu.SemaphoreType.DMA((COPIES,))],
        compiler_params=pltpu.CompilerParams(vmem_limit_bytes=44 * 2**20),
        cost_estimate=pl.CostEstimate(flops=2 * sensors * modes, bytes_accessed=12 * sensors * modes, transcendentals=sensors),
        name="prepare",
    )
    block_row = block_of_sensor.reshape(1, sensors)
    rate_row = mode_rate.reshape(1, modes)
    var_row = mode_var.reshape(1, modes)

    pieces, prepared = exchange(
        observations,
        block_mask,
        count,
        lambda noise: sensor_basis * lax.rsqrt(noise)[:, None],
        lambda scaled: prepare(scaled, block_row, rate_row, var_row),
        noise_var,
    )
    scaled_t, scaled, onehot, coefs = prepared

    square = pltpu.VMEM((modes, modes), F32)
    field, variances, misfit = pl.pallas_call(
        functools.partial(filter_kernel, count=count, local=local, blocks=blocks, parts=len(pieces)),
        out_shape=(
            jax.ShapeDtypeStruct((local, sensors), F32),
            jax.ShapeDtypeStruct((local, 2 * modes), F32),
            jax.ShapeDtypeStruct((1, 1), F32),
        ),
        in_specs=[pl.BlockSpec(memory_space=pltpu.SMEM)] + in_vmem(len(pieces) + 5),
        out_specs=tuple(in_vmem(3)),
        scratch_shapes=[
            square,
            square,
            square,
            square,
            pltpu.VMEM((2, modes, modes), F32),
            pltpu.VMEM((4, modes, modes), F32),
            square,
            pltpu.VMEM((1, sensors), F32),
            pltpu.VMEM((steps, sensors), F32),
            pltpu.VMEM((steps, sensors), F32),
            pltpu.VMEM((steps, modes), F32),
            pltpu.VMEM((steps, modes), F32),
            pltpu.VMEM((steps, 2 * modes), F32),
            pltpu.VMEM((8, modes), F32),
            pltpu.VMEM((steps, LANES), F32),
            pltpu.VMEM((2 * modes, 2 * modes), F32),
            pltpu.VMEM((1, 2 * modes), F32),
            pltpu.VMEM((1, modes), F32),
        ],
        compiler_params=pltpu.CompilerParams(vmem_limit_bytes=20 * 2**20),
        cost_estimate=pl.CostEstimate(flops=steps * sensors * modes * 512, bytes_accessed=8 * sensors * modes, transcendentals=0),
        name="filter",
    )(position.reshape(1), *pieces, onehot, scaled_t, scaled, noise_row, coefs)

    return (field, variances, misfit.reshape(1))


def solution(mesh):
    in_specs = (P(("groups", "tm"), None), P(("groups", "tm"), None), P(), P(), P(), P(), P())
    out_specs = (P(("groups", "tm"), None), P(("groups", "tm"), None), P("groups"))
    return jax.shard_map(on_device, mesh=mesh, in_specs=in_specs, out_specs=out_specs, check_vma=False)
```
